512 devices in a mesh: slab: 8 (over y_lo, x), dp: 64 (over y_hi, z, core).
Axes of the slice: x: 4, y: 8 (y_hi: 4, y_lo: 2; y = y_hi * 2 + y_lo), z: 8, core: 2. Of those that a mesh axis runs over, the one named last changes fastest.
Arguments:
- activations: bfloat16 [64, 32, 16, 4096], P('dp', 'slab'), may hold values from -6 to 6
- cotangent: bfloat16 [64, 32, 16, 4096], P('dp', 'slab'), may hold values from -6 to 6
- params: float32 [110592], P(('slab', 'dp')), may hold values from -0.15625 to 0.15625
- moment_one: float32 [110592], P(('slab', 'dp')), may hold values from -0.6 to 0.6
- moment_two: float32 [110592], P(('slab', 'dp')), may hold values from 0.004 to 0.04
Outputs:
- result: bfloat16 [64, 32, 16, 4096], P('dp', 'slab')
- input_grad: bfloat16 [64, 32, 16, 4096], P('dp', 'slab')
- new_params: float32 [110592], P(('slab', 'dp'))
- new_moment_one: float32 [110592], P(('slab', 'dp'))
- new_moment_two: float32 [110592], P(('slab', 'dp'))
The draws below stay inside these ranges and needn't reach their ends.
All inputs are finite; a program needn't handle non-finite values.
Results may differ from the reference program's by a relative error of at most 0.008.
Values may be sent and summed in bfloat16 or wider, within the bound.
A program may use at most 64 MiB of HBM per device.

```python
import math
import jax
import jax.numpy as jnp
from jax import lax

C = 64
NX = 64
NY = 16
NZ = 32
BATCH = 64
W_TOTAL = 110592


def steps_of(key, dims, pieces, low, largest):
    gain = 1.0
    for axis_at, shards_of in pieces:
        heights = jax.random.uniform(jax.random.fold_in(jax.random.fold_in(key, 6), axis_at), (shards_of,), jnp.float32, low / len(pieces), largest / len(pieces))
        gain = gain * jnp.repeat(jnp.exp(heights), dims[axis_at] // shards_of).reshape((-1,) + (1,) * (len(dims) - 1 - axis_at))
    return gain


def scatter_about(rng, dims, spread, limit, pieces=(), dtype=jnp.bfloat16):
    gain = steps_of(rng, dims, pieces, -0.22, 0.18) if pieces else 1.0
    values = jax.random.normal(rng, dims, jnp.float32) * spread * gain
    return jnp.minimum(jnp.maximum(values, -limit), limit).astype(dtype)


def setup_inputs(seed: int = 0) -> dict:
    splits = jax.random.split(jax.random.key(seed), 6)
    return {
        "activations": scatter_about(splits[0], (BATCH, NZ, NY, NX * C), 1.0, 6.0, ((0, 64), (1, 8))),
        "cotangent": scatter_about(splits[1], (BATCH, NZ, NY, NX * C), 1.0, 6.0, ((0, 64), (1, 8))),
        "params": scatter_about(splits[2], (W_TOTAL,), (27 * C) ** -0.5, 0.15625, ((0, 512),), jnp.float32),
        "moment_one": scatter_about(splits[3], (W_TOTAL,), 0.1, 0.6, ((0, 512),), jnp.float32),
        "moment_two": jnp.clip(jnp.exp(math.log(0.04) - 2.30258502 * jax.random.uniform(splits[4], (W_TOTAL,), jnp.float32) ** steps_of(splits[4], (W_TOTAL,), ((0, 512),), -0.2, 0.2)), 0.004, 0.04),
    }


def convolve(field, kernel):
    return lax.conv_general_dilated(field, kernel, (1, 1, 1), 'SAME', dimension_numbers=('NDHWC', 'DHWIO', 'NDHWC'), precision=lax.Precision.HIGHEST)

def reference(activations, cotangent, params, moment_one, moment_two):
    rounded = lax.optimization_barrier(params.astype(jnp.bfloat16))
    kernel = rounded.astype(jnp.float32).reshape(3, 3, 3, C, C)

    def one_sample(total, pair):
        field = pair[0].astype(jnp.float32).reshape(1, NZ, NY, NX, C)
        seed_grad = pair[1].astype(jnp.float32).reshape(1, NZ, NY, NX, C)
        output, pull = jax.vjp(convolve, field, kernel)
        field_grad, kernel_grad = pull(seed_grad)
        return (total + kernel_grad, (output.reshape(NZ, NY, NX * C).astype(jnp.bfloat16), field_grad.reshape(NZ, NY, NX * C).astype(jnp.bfloat16)))
    start = jnp.zeros((3, 3, 3, C, C), jnp.float32)
    total, outputs = lax.scan(one_sample, start, (activations, cotangent))
    cells = BATCH * NZ * NY * NX
    grad = total.reshape(-1) / jnp.sqrt(jnp.float32(cells))
    new_one = 0.9 * moment_one + 0.1 * grad
    new_two = 0.999 * moment_two + 0.001 * grad * grad
    step = 3.0 * (new_one / (1.0 - 0.9 ** 10)) / (jnp.sqrt(new_two / (1.0 - 0.999 ** 10)) + 1e-08)
    return (outputs[0], outputs[1], params - step, new_one, new_two)
```

```python
import jax
import jax.numpy as jnp
from jax import lax
from jax.experimental import pallas as pl
from jax.experimental.pallas import tpu as pltpu
from jax.sharding import PartitionSpec as P

MESH = pl.DeviceIdType.MESH
F32 = jnp.float32
BF16 = jnp.bfloat16
SHARE = 216
PLANE = 512


def place():
    slab, dp = lax.axis_index("slab"), lax.axis_index("dp")
    return {
        "slab": slab,
        "dp": dp,
        "t": slab // 2,
        "u": (slab % 2) * 4 + dp // 16,
        "z": (dp // 2) % 8,
        "core": dp % 2,
    }


def u_peer(me, d):
    other = (me["u"] + d) % 8
    return ((me["slab"] // 2) * 2 + other // 4, (other % 4) * 16 + me["dp"] % 16)


def t_peer(me, d):
    return (((me["t"] + d) % 4) * 2 + me["slab"] % 2, me["dp"])


def z_peer(me, d):
    return (me["slab"], (me["dp"] // 16) * 16 + ((me["z"] + d) % 8) * 2 + me["core"])


def core_peer(me):
    return (me["slab"], me["dp"] + 1 - 2 * me["core"])


def slab_peer(me, d):
    return ((me["slab"] + d) % 8, me["dp"])


def greet(peers):
    barrier = pltpu.get_barrier_semaphore()
    for peer in peers:
        pl.semaphore_signal(barrier, inc=1, device_id=peer, device_id_type=MESH)
    pl.semaphore_wait(barrier, len(peers))


def share_peers(me):
    return (
        [u_peer(me, d) for d in range(1, 8)]
        + [t_peer(me, d) for d in range(1, 4)]
        + [z_peer(me, d) for d in range(1, 8)]
        + [core_peer(me)]
    )


def remote(src, dst, sems, index, peer):
    return pltpu.make_async_remote_copy(
        src_ref=src,
        dst_ref=dst,
        send_sem=sems.at[0, index],
        recv_sem=sems.at[1, index],
        device_id=peer,
        device_id_type=MESH,
    )


def start(copies):
    for copy in copies:
        copy.start()
    return copies


def wait_recv(copies):
    for copy in copies:
        copy.wait_recv()


def wait_send(copies):
    for copy in copies:
        copy.wait_send()


def iota(shape, axis):
    return lax.broadcasted_iota(jnp.int32, shape, axis)


def gather_kernel(act, cot, par, act_pad, cot_pad, weights, act_buf, cot_buf, row, rows, tiles, wide, local, hs, us, ts, zs, cs):
    me = place()
    greet(share_peers(me) + [slab_peer(me, 1), slab_peer(me, 7)])
    row[...] = jnp.zeros_like(row)
    row[0:1, 0:SHARE] = par[...]
    own = jnp.broadcast_to(row[0:1, :], (8, 256))
    row[...] = jnp.where(iota((8, 256), 0) == me["u"], own, 0.0)
    first = start([remote(row, rows.at[d - 1], us, d - 1, u_peer(me, d)) for d in range(1, 8)])
    halo = []
    for k, (src, buf) in enumerate(((act, act_buf), (cot, cot_buf))):
        halo.append(remote(src.at[3], buf.at[0], hs, 2 * k, slab_peer(me, 1)))
        halo.append(remote(src.at[0], buf.at[5], hs, 2 * k + 1, slab_peer(me, 7)))
    start(halo)
    inner = []
    for k, (src, pad) in enumerate(((act, act_pad), (cot, cot_pad))):
        inner.append(pltpu.make_async_copy(src, pad.at[pl.ds(1, 4)], local.at[k]))
    start(inner)
    wait_recv(first)
    tile = row[...]
    for d in range(7):
        tile = tile + rows[d]
    tiles[me["t"]] = tile
    second = start([remote(tiles.at[me["t"]], tiles.at[me["t"]], ts, d - 1, t_peer(me, d)) for d in range(1, 4)])
    wait_recv(second)
    wide[me["core"], me["z"]] = jnp.concatenate([tiles[k] for k in range(4)], axis=0).astype(BF16)
    mine = wide.at[me["core"], me["z"]]
    third = start([remote(mine, mine, zs, d - 1, z_peer(me, d)) for d in range(1, 8)])
    wait_recv(third)
    half = wide.at[me["core"]]
    fourth = start([remote(half, half, cs, 0, core_peer(me))])
    wait_recv(halo)
    for buf, pad in ((act_buf, act_pad), (cot_buf, cot_pad)):
        low, high = buf[0], buf[5]
        pad[0] = jnp.where(me["slab"] == 0, jnp.zeros_like(low), low)
        pad[5] = jnp.where(me["slab"] == 7, jnp.zeros_like(high), high)
    wait_recv(fourth)
    weights[...] = wide[...]
    for copy in inner:
        copy.wait()
    wait_send(first + halo + second + third + fourth)


def gather(act, cot, par):
    vmem = pl.BlockSpec(memory_space=pltpu.VMEM)
    planes = jax.ShapeDtypeStruct((6, 16, 4096), BF16)
    return pl.pallas_call(
        gather_kernel,
        out_shape=(planes, planes, jax.ShapeDtypeStruct((2, 8, 32, 256), BF16)),
        in_specs=[vmem] * 3,
        out_specs=(vmem,) * 3,
        scratch_shapes=[
            pltpu.VMEM((6, 16, 4096), BF16),
            pltpu.VMEM((6, 16, 4096), BF16),
            pltpu.VMEM((8, 256), F32),
            pltpu.VMEM((7, 8, 256), F32),
            pltpu.VMEM((4, 8, 256), F32),
            pltpu.VMEM((2, 8, 32, 256), BF16),
            pltpu.SemaphoreType.DMA((2,)),
            pltpu.SemaphoreType.DMA((2, 4)),
            pltpu.SemaphoreType.DMA((2, 7)),
            pltpu.SemaphoreType.DMA((2, 3)),
            pltpu.SemaphoreType.DMA((2, 7)),
            pltpu.SemaphoreType.DMA((2, 1)),
        ],
        compiler_params=pltpu.CompilerParams(
            collective_id=0, has_side_effects=True, vmem_limit_bytes=32 * 2**20
        ),
    )(act, cot, par)


def spread(field, out, p):
    moved = pltpu.roll(field[p].astype(F32), 64, 1)
    lane = iota((16, 128), 1)
    line = iota((16, 128), 0)
    base = p * PLANE if isinstance(p, int) else pl.multiple_of(p * PLANE, PLANE)
    for chunk in range(33):
        if chunk == 0:
            cells = jnp.where(lane >= 64, moved[:, 0:128], 0.0)
        elif chunk == 32:
            cells = jnp.where(lane < 64, moved[:, 0:128], 0.0)
        else:
            cells = moved[:, 128 * chunk : 128 * chunk + 128]
        above = jnp.where(line > 0, pltpu.roll(cells, 1, 0), 0.0)
        below = jnp.where(line < 15, pltpu.roll(cells, 15, 0), 0.0)
        for ky, part in enumerate((above, cells, below)):
            part = part.astype(BF16)
            if chunk < 32:
                out[pl.ds(base + 16 * chunk, 16), 256 * ky : 256 * ky + 128] = part
            if chunk > 0:
                out[pl.ds(base + 16 * (chunk - 1), 16), 256 * ky + 128 : 256 * ky + 256] = part


def turn(field, out, p):
    plane = field[p]
    stacked = jnp.concatenate([plane[:, 128 * g : 128 * g + 128] for g in range(32)], axis=0)
    out[pl.ds((p - 1) * 128, 128), :] = stacked.T


def kernel_gradient(turned, spread_cot, total):
    for p in (2, 3, 1, 4, 0, 5):
        low, high = max(0, 2 - p), min(2, 5 - p)
        first, count = p - 2 + low, high - low + 1
        term = jnp.dot(
            turned[first * 128 : (first + count) * 128, :],
            spread_cot[p * PLANE : (p + 1) * PLANE, :],
            preferred_element_type=F32,
        )
        if p == 2:
            total[...] = term
        else:
            total[low * 128 : (high + 1) * 128, :] += term


def fold(total, flat):
    for kz in range(3):
        for ky in range(3):
            at = 256 * (2 - ky)
            left = total[kz * 128 : kz * 128 + 64, at : at + 256]
            right = total[kz * 128 + 64 : kz * 128 + 128, at : at + 256]
            both = left + pltpu.roll(right, 192, 1)
            row = (kz * 3 + ky) * 3 * 64
            flat[row : row + 64, :] = both[:, 128:256]
            flat[row + 64 : row + 128, :] = pltpu.roll(both[:, 0:128], 64, 1)
            flat[row + 128 : row + 192, :] = both[:, 0:128]


def to_shares(flat, shares):
    lane = iota((32, 128), 1)
    for zh in range(2):
        source = [flat[pl.ds(27 * zh + r, 32, stride=54), :] for r in range(27)]
        for s in range(8):
            halves = [jnp.zeros((32, 128), F32), jnp.zeros((32, 128), F32)]
            for r in range(SHARE * s // 64, (SHARE * s + SHARE - 1) // 64 + 1):
                at = 64 * r - SHARE * s
                moved = pltpu.roll(source[r], at % 128, 1) if at % 128 else source[r]
                low, high = max(at, 0), min(at + 64, SHARE)
                for h in range(2):
                    begin, end = max(low - 128 * h, 0), min(high - 128 * h, 128)
                    if begin < end:
                        halves[h] = jnp.where((lane >= begin) & (lane < end), moved, halves[h])
            for h in range(2):
                shares[s % 2, zh * 4 + s // 2, :, 128 * h : 128 * h + 128] = halves[h]


def from_shares(shares, flat):
    lane = iota((32, 128), 1)
    for zh in range(2):
        source = [
            [shares[s % 2, zh * 4 + s // 2, :, 128 * h : 128 * h + 128].astype(F32) for h in range(2)]
            for s in range(8)
        ]
        for r in range(27):
            out = jnp.zeros((32, 128), F32)
            for s in range(64 * r // SHARE, (64 * r + 63) // SHARE + 1):
                shift = SHARE * s - 64 * r
                low, high = max(64 * r, SHARE * s) - SHARE * s, min(64 * r + 64, SHARE * (s + 1)) - SHARE * s
                for h in range(2):
                    begin, end = max(low, 128 * h), min(high, 128 * h + 128)
                    if begin < end:
                        by = (shift + 128 * h) % 128
                        moved = pltpu.roll(source[s][h], by, 1) if by else source[s][h]
                        out = jnp.where((lane >= begin + shift) & (lane < end + shift), moved, out)
            flat[pl.ds(27 * zh + r, 32, stride=54), :] = out


def bands(flat, forward, backward):
    for kz in range(3):
        for ky in range(3):
            row = (kz * 3 + ky) * 3 * 64
            taps = [flat[row + 64 * kx : row + 64 * kx + 64, :] for kx in range(3)]
            moved = [pltpu.roll(tap, 64, 1) for tap in taps]
            at = kz * 768 + ky * 256
            blocks = (taps[0], taps[1] + moved[0], taps[2] + moved[1], moved[2])
            forward[at : at + 256, :] = jnp.concatenate(blocks, axis=0).astype(BF16)
            at = (2 - kz) * 768 + (2 - ky) * 256
            left = jnp.concatenate([taps[2] + moved[1], moved[2]], axis=0)
            right = jnp.concatenate([taps[0], taps[1] + moved[0]], axis=0)
            backward[at : at + 128, :] = left.T.astype(BF16)
            backward[at + 128 : at + 256, :] = right.T.astype(BF16)


def convolve(spread_field, band, out, z):
    total = None
    for kz in range(3):
        at = (z + kz) * PLANE if isinstance(z, int) else pl.multiple_of((z + kz) * PLANE, PLANE)
        term = jnp.dot(
            spread_field[pl.ds(at, PLANE), :],
            band[kz * 768 : kz * 768 + 768, :],
            preferred_element_type=F32,
        )
        total = term if total is None else total + term
    rounded = total.astype(BF16)
    for g in range(32):
        out[z, :, 128 * g : 128 * g + 128] = rounded[16 * g : 16 * g + 16, :]


def compute_kernel(act, cot, weights, result, input_grad, shares, a3, b3, turned, total, flat, forward, backward):
    @pl.loop(0, 6)
    def _(p):
        spread(act, a3, p)
        spread(cot, b3, p)

    for p in range(1, 5):
        turn(act, turned, p)
    kernel_gradient(turned, b3, total)
    fold(total, flat)
    to_shares(flat, shares)
    from_shares(weights, flat)
    bands(flat, forward, backward)

    @pl.loop(0, 4)
    def _(z):
        convolve(a3, forward, result, z)
        convolve(b3, backward, input_grad, z)


def compute(act, cot, weights):
    vmem = pl.BlockSpec(memory_space=pltpu.VMEM)
    planes = jax.ShapeDtypeStruct((4, 16, 4096), BF16)
    return pl.pallas_call(
        compute_kernel,
        out_shape=(planes, planes, jax.ShapeDtypeStruct((2, 8, 32, 256), F32)),
        in_specs=[vmem] * 3,
        out_specs=(vmem,) * 3,
        scratch_shapes=[
            pltpu.VMEM((6 * PLANE, 768), BF16),
            pltpu.VMEM((6 * PLANE, 768), BF16),
            pltpu.VMEM((512, 512), BF16),
            pltpu.VMEM((384, 768), F32),
            pltpu.VMEM((1728, 128), F32),
            pltpu.VMEM((2304, 128), BF16),
            pltpu.VMEM((2304, 128), BF16),
        ],
        compiler_params=pltpu.CompilerParams(vmem_limit_bytes=48 * 2**20),
    )(act, cot, weights)


def update_kernel(shares, par, one, two, new_par, new_one, new_two, got, mine, sent, parts, tile, tiles, row, rows, us, ts, zs, cs):
    me = place()
    greet(share_peers(me))
    first = start([remote(shares.at[1 - me["core"]], got, cs, 0, core_peer(me))])
    wait_recv(first)
    for k in range(8):
        both = shares[me["core"], k] + got[k]
        mine[k] = both
        sent[k] = both.astype(BF16)
    second = start(
        [remote(sent.at[(me["z"] + d) % 8], parts.at[d - 1], zs, d - 1, z_peer(me, d)) for d in range(1, 8)]
    )
    wait_recv(second)
    total = mine[me["z"]]
    for d in range(7):
        total = total + parts[d].astype(F32)
    for k in range(4):
        tile[k] = total[8 * k : 8 * k + 8, :]
    third = start([remote(tile.at[(me["t"] + d) % 4], tiles.at[d - 1], ts, d - 1, t_peer(me, d)) for d in range(1, 4)])
    wait_recv(third)
    row[...] = tile[me["t"]] + tiles[0] + tiles[1] + tiles[2]
    fourth = start([remote(row, rows.at[d - 1], us, d - 1, u_peer(me, d)) for d in range(1, 8)])
    wait_recv(fourth)
    total = row[...]
    for d in range(7):
        total = total + rows[d]
    share = jnp.sum(jnp.where(iota((8, 256), 0) == me["u"], total, 0.0), axis=0, keepdims=True)
    grad = share[:, 0:SHARE] / jnp.sqrt(F32(64 * 32 * 16 * 64))
    first_moment = 0.9 * one[...] + 0.1 * grad
    second_moment = 0.999 * two[...] + 0.001 * grad * grad
    step = 3.0 * (first_moment / (1.0 - 0.9**10)) / (jnp.sqrt(second_moment / (1.0 - 0.999**10)) + 1e-08)
    new_par[...] = par[...] - step
    new_one[...] = first_moment
    new_two[...] = second_moment
    wait_send(first + second + third + fourth)


def update(shares, par, one, two):
    vmem = pl.BlockSpec(memory_space=pltpu.VMEM)
    share = jax.ShapeDtypeStruct((1, SHARE), F32)
    return pl.pallas_call(
        update_kernel,
        out_shape=(share,) * 3,
        in_specs=[vmem] * 4,
        out_specs=(vmem,) * 3,
        scratch_shapes=[
            pltpu.VMEM((8, 32, 256), F32),
            pltpu.VMEM((8, 32, 256), F32),
            pltpu.VMEM((8, 32, 256), BF16),
            pltpu.VMEM((7, 32, 256), BF16),
            pltpu.VMEM((4, 8, 256), F32),
            pltpu.VMEM((3, 8, 256), F32),
            pltpu.VMEM((8, 256), F32),
            pltpu.VMEM((7, 8, 256), F32),
            pltpu.SemaphoreType.DMA((2, 7)),
            pltpu.SemaphoreType.DMA((2, 3)),
            pltpu.SemaphoreType.DMA((2, 7)),
            pltpu.SemaphoreType.DMA((2, 1)),
        ],
        compiler_params=pltpu.CompilerParams(
            collective_id=1, has_side_effects=True, vmem_limit_bytes=32 * 2**20
        ),
    )(shares, par, one, two)


def on_device(activations, cotangent, params, moment_one, moment_two):
    act, cot = activations[0], cotangent[0]
    par, one, two = (a.reshape(1, SHARE) for a in (params, moment_one, moment_two))
    act_pad, cot_pad, weights = gather(act, cot, par)
    result, input_grad, shares = compute(act_pad, cot_pad, weights)
    new_par, new_one, new_two = update(shares, par, one, two)
    return (
        result[None],
        input_grad[None],
        new_par.reshape(SHARE),
        new_one.reshape(SHARE),
        new_two.reshape(SHARE),
    )


def solution(mesh):
    field, share = P("dp", "slab", None, None), P(("slab", "dp"))
    return jax.shard_map(
        on_device,
        mesh=mesh,
        in_specs=(field, field, share, share, share),
        out_specs=(field, field, share, share, share),
        check_vma=False,
    )
```

```python
import jax
import jax.numpy as jnp
from jax import lax
from jax.experimental import pallas as pl
from jax.experimental.pallas import tpu as pltpu
from jax.sharding import PartitionSpec as P

MESH = pl.DeviceIdType.MESH
F32 = jnp.float32
BF16 = jnp.bfloat16
SHARE = 216
PLANE = 512


def place():
    slab, dp = lax.axis_index("slab"), lax.axis_index("dp")
    return {
        "slab": slab,
        "dp": dp,
        "x": slab % 4,
        "y": (dp // 16) * 2 + slab // 4,
        "row": slab * 4 + dp // 16,
        "z": (dp // 2) % 8,
        "core": dp % 2,
    }


def hops(d, n):
    return min(d, n - d)


XY = sorted(
    [(dx, dy) for dx in range(4) for dy in range(8) if dx or dy],
    key=lambda o: -(hops(o[0], 4) + hops(o[1], 8)),
)
Z = sorted(range(1, 8), key=lambda d: -hops(d, 8))


def xy_peer(me, offset):
    x, y = (me["x"] + offset[0]) % 4, (me["y"] + offset[1]) % 8
    return ((y % 2) * 4 + x, (y // 2) * 16 + me["dp"] % 16)


def xy_row(me, offset):
    slab, dp = xy_peer(me, offset)
    return slab * 4 + dp // 16


def z_peer(me, d):
    return (me["slab"], (me["dp"] // 16) * 16 + ((me["z"] + d) % 8) * 2 + me["core"])


def core_peer(me):
    return (me["slab"], me["dp"] + 1 - 2 * me["core"])


def slab_peer(me, d):
    return ((me["slab"] + d) % 8, me["dp"])


def remote(src, dst, sems, index, peer):
    return pltpu.make_async_remote_copy(
        src_ref=src,
        dst_ref=dst,
        send_sem=sems.at[0, index],
        recv_sem=sems.at[1, index],
        device_id=peer,
        device_id_type=MESH,
    )


def start(copies):
    for copy in copies:
        copy.start()
    return copies


def wait_recv(copies):
    for copy in copies:
        copy.wait_recv()


def wait_send(copies):
    for copy in copies:
        copy.wait_send()


def iota(shape, axis):
    return lax.broadcasted_iota(jnp.int32, shape, axis)


def spread(field, out, p, keep=None):
    moved = pltpu.roll(field[p].astype(F32), 64, 1)
    if keep is not None:
        moved = jnp.where(keep, moved, 0.0)
    lane = iota((16, 128), 1)
    line = iota((16, 128), 0)
    base = p * PLANE if isinstance(p, int) else pl.multiple_of(p * PLANE, PLANE)
    for chunk in range(33):
        if chunk == 0:
            cells = jnp.where(lane >= 64, moved[:, 0:128], 0.0)
        elif chunk == 32:
            cells = jnp.where(lane < 64, moved[:, 0:128], 0.0)
        else:
            cells = moved[:, 128 * chunk : 128 * chunk + 128]
        above = jnp.where(line > 0, pltpu.roll(cells, 1, 0), 0.0)
        below = jnp.where(line < 15, pltpu.roll(cells, 15, 0), 0.0)
        for ky, part in enumerate((above, cells, below)):
            part = part.astype(BF16)
            if chunk < 32:
                out[pl.ds(base + 16 * chunk, 16), 256 * ky : 256 * ky + 128] = part
            if chunk > 0:
                out[pl.ds(base + 16 * (chunk - 1), 16), 256 * ky + 128 : 256 * ky + 256] = part


def turn(field, out, p):
    plane = field[p]
    stacked = jnp.concatenate([plane[:, 128 * g : 128 * g + 128] for g in range(32)], axis=0)
    out[pl.ds((p - 1) * 128, 128), :] = stacked.T


def kernel_gradient(turned, spread_cot, total, planes):
    for p in planes:
        low, high = max(0, 2 - p), min(2, 5 - p)
        first, count = p - 2 + low, high - low + 1
        term = jnp.dot(
            turned[first * 128 : (first + count) * 128, :],
            spread_cot[p * PLANE : (p + 1) * PLANE, :],
            preferred_element_type=F32,
        )
        if p == 2:
            total[...] = term
        else:
            total[low * 128 : (high + 1) * 128, :] += term


def fold(total, flat):
    for kz in range(3):
        for ky in range(3):
            at = 256 * (2 - ky)
            left = total[kz * 128 : kz * 128 + 64, at : at + 256]
            right = total[kz * 128 + 64 : kz * 128 + 128, at : at + 256]
            both = left + pltpu.roll(right, 192, 1)
            row = (kz * 3 + ky) * 3 * 64
            flat[row : row + 64, :] = both[:, 128:256]
            flat[row + 64 : row + 128, :] = pltpu.roll(both[:, 0:128], 64, 1)
            flat[row + 128 : row + 192, :] = both[:, 0:128]


def to_shares(flat, shares):
    lane = iota((32, 128), 1)
    for zh in range(2):
        source = [flat[pl.ds(27 * zh + r, 32, stride=54), :] for r in range(27)]
        for s in range(8):
            halves = [jnp.zeros((32, 128), F32), jnp.zeros((32, 128), F32)]
            for r in range(SHARE * s // 64, (SHARE * s + SHARE - 1) // 64 + 1):
                at = 64 * r - SHARE * s
                moved = pltpu.roll(source[r], at % 128, 1) if at % 128 else source[r]
                low, high = max(at, 0), min(at + 64, SHARE)
                for h in range(2):
                    begin, end = max(low - 128 * h, 0), min(high - 128 * h, 128)
                    if begin < end:
                        halves[h] = jnp.where((lane >= begin) & (lane < end), moved, halves[h])
            for h in range(2):
                shares[s % 2, zh * 4 + s // 2, :, 128 * h : 128 * h + 128] = halves[h]


def from_shares(shares, flat):
    lane = iota((32, 128), 1)
    for zh in range(2):
        source = [
            [shares[s % 2, zh * 4 + s // 2, :, 128 * h : 128 * h + 128].astype(F32) for h in range(2)]
            for s in range(8)
        ]
        for r in range(27):
            out = jnp.zeros((32, 128), F32)
            for s in range(64 * r // SHARE, (64 * r + 63) // SHARE + 1):
                shift = SHARE * s - 64 * r
                low, high = max(64 * r, SHARE * s) - SHARE * s, min(64 * r + 64, SHARE * (s + 1)) - SHARE * s
                for h in range(2):
                    begin, end = max(low, 128 * h), min(high, 128 * h + 128)
                    if begin < end:
                        by = (shift + 128 * h) % 128
                        moved = pltpu.roll(source[s][h], by, 1) if by else source[s][h]
                        out = jnp.where((lane >= begin + shift) & (lane < end + shift), moved, out)
            flat[pl.ds(27 * zh + r, 32, stride=54), :] = out


def bands(flat, forward, backward):
    for kz in range(3):
        for ky in range(3):
            row = (kz * 3 + ky) * 3 * 64
            taps = [flat[row + 64 * kx : row + 64 * kx + 64, :] for kx in range(3)]
            moved = [pltpu.roll(tap, 64, 1) for tap in taps]
            at = kz * 768 + ky * 256
            blocks = (taps[0], taps[1] + moved[0], taps[2] + moved[1], moved[2])
            forward[at : at + 256, :] = jnp.concatenate(blocks, axis=0).astype(BF16)
            at = (2 - kz) * 768 + (2 - ky) * 256
            left = jnp.concatenate([taps[2] + moved[1], moved[2]], axis=0)
            right = jnp.concatenate([taps[0], taps[1] + moved[0]], axis=0)
            backward[at : at + 128, :] = left.T.astype(BF16)
            backward[at + 128 : at + 256, :] = right.T.astype(BF16)


def convolve(spread_field, band, out, z):
    total = None
    for kz in range(3):
        at = (z + kz) * PLANE if isinstance(z, int) else pl.multiple_of((z + kz) * PLANE, PLANE)
        term = jnp.dot(
            spread_field[pl.ds(at, PLANE), :],
            band[kz * 768 : kz * 768 + 768, :],
            preferred_element_type=F32,
        )
        total = term if total is None else total + term
    rounded = total.astype(BF16)
    for g in range(32):
        out[z, :, 128 * g : 128 * g + 128] = rounded[16 * g : 16 * g + 16, :]


def step_kernel(
    act, cot, par, result, input_grad, grad,
    act_pad, cot_pad, share, row, rows, wide,
    a3, b3, turned, total, flat, forward, backward,
    shares, got, mine, sent, parts, terms, term_parts,
    local, hs, gx, gz, gc, rc, rz, rx,
):
    me = place()
    barrier = pltpu.get_barrier_semaphore()
    peers = (
        [xy_peer(me, o) for o in XY]
        + [z_peer(me, d) for d in Z]
        + [core_peer(me), slab_peer(me, 1), slab_peer(me, 7)]
    )
    for peer in peers:
        pl.semaphore_signal(barrier, inc=1, device_id=peer, device_id_type=MESH)
    inner = start([
        pltpu.make_async_copy(cot, cot_pad.at[pl.ds(1, 4)], local.at[0]),
        pltpu.make_async_copy(act, act_pad.at[pl.ds(1, 4)], local.at[1]),
        pltpu.make_async_copy(par, share, local.at[2]),
    ])
    inner[0].wait()

    @pl.loop(1, 5)
    def _(p):
        spread(cot_pad, b3, p)

    inner[1].wait()
    for p in range(1, 5):
        turn(act_pad, turned, p)
    inner[2].wait()
    row[...] = jnp.zeros_like(row)
    row[0, :, 0:SHARE] = share[...]
    rows[me["row"]] = row[0]
    pl.semaphore_wait(barrier, len(peers))

    cot_halo = start([
        remote(cot_pad.at[4], cot_pad.at[0], hs, 0, slab_peer(me, 1)),
        remote(cot_pad.at[1], cot_pad.at[5], hs, 1, slab_peer(me, 7)),
    ])
    own = rows.at[me["row"]]
    gather_xy = start([remote(row.at[0], own, gx, k, xy_peer(me, o)) for k, o in enumerate(XY)])
    act_halo = start([
        remote(act_pad.at[4], act_pad.at[0], hs, 2, slab_peer(me, 1)),
        remote(act_pad.at[1], act_pad.at[5], hs, 3, slab_peer(me, 7)),
    ])

    @pl.loop(1, 5)
    def _(p):
        spread(act_pad, a3, p)

    kernel_gradient(turned, b3, total, (2, 3, 1, 4))

    wait_recv(gather_xy)
    wide[me["core"], me["z"]] = jnp.concatenate([rows[k] for k in range(32)], axis=0).astype(BF16)
    block = wide.at[me["core"], me["z"]]
    gather_z = start([remote(block, block, gz, k, z_peer(me, d)) for k, d in enumerate(Z)])

    def edges(pad, out):
        @pl.loop(0, 2)
        def _(k):
            spread(pad, out, 5 * k, me["slab"] != 7 * k)

    wait_recv(cot_halo)
    edges(cot_pad, b3)
    kernel_gradient(turned, b3, total, (0, 5))
    fold(total, flat)
    to_shares(flat, shares)
    sum_core = start([remote(shares.at[1 - me["core"]], got, rc, 0, core_peer(me))])

    wait_recv(act_halo)
    edges(act_pad, a3)
    wait_recv(sum_core)
    for k in range(8):
        both = shares[me["core"], k] + got[k]
        mine[k] = both
        sent[k] = both.astype(BF16)
    sum_z = start([remote(sent.at[(me["z"] + d) % 8], parts.at[k], rz, k, z_peer(me, d)) for k, d in enumerate(Z)])

    wait_recv(gather_z)
    half = wide.at[me["core"]]
    gather_core = start([remote(half, half, gc, 0, core_peer(me))])
    wait_recv(gather_core)
    from_shares(wide, flat)
    bands(flat, forward, backward)

    @pl.loop(0, 4)
    def _(z):
        convolve(a3, forward, result, z)

    wait_recv(sum_z)
    summed = mine[me["z"]]
    for k in range(7):
        summed = summed + parts[k].astype(F32)
    for k in range(32):
        terms[k] = summed[k : k + 1, :]
    sum_xy = start([
        remote(terms.at[xy_row(me, o)], term_parts.at[k], rx, k, xy_peer(me, o)) for k, o in enumerate(XY)
    ])

    @pl.loop(0, 4)
    def _(z):
        convolve(b3, backward, input_grad, z)

    wait_recv(sum_xy)
    summed = terms[me["row"]]
    for k in range(31):
        summed = summed + term_parts[k]
    grad[...] = summed
    wait_send(cot_halo + gather_xy + act_halo + gather_z + sum_core + sum_z + gather_core + sum_xy)


def step(act, cot, par):
    vmem, hbm = pl.BlockSpec(memory_space=pltpu.VMEM), pl.BlockSpec(memory_space=pltpu.HBM)
    planes = jax.ShapeDtypeStruct((4, 16, 4096), BF16)
    return pl.pallas_call(
        step_kernel,
        out_shape=(planes, planes, jax.ShapeDtypeStruct((1, 256), F32)),
        in_specs=[hbm] * 3,
        out_specs=(vmem,) * 3,
        scratch_shapes=[
            pltpu.VMEM((6, 16, 4096), BF16),
            pltpu.VMEM((6, 16, 4096), BF16),
            pltpu.VMEM((1, SHARE), F32),
            pltpu.VMEM((1, 1, 256), F32),
            pltpu.VMEM((32, 1, 256), F32),
            pltpu.VMEM((2, 8, 32, 256), BF16),
            pltpu.VMEM((6 * PLANE, 768), BF16),
            pltpu.VMEM((6 * PLANE, 768), BF16),
            pltpu.VMEM((512, 512), BF16),
            pltpu.VMEM((384, 768), F32),
            pltpu.VMEM((1728, 128), F32),
            pltpu.VMEM((2304, 128), BF16),
            pltpu.VMEM((2304, 128), BF16),
            pltpu.VMEM((2, 8, 32, 256), F32),
            pltpu.VMEM((8, 32, 256), F32),
            pltpu.VMEM((8, 32, 256), F32),
            pltpu.VMEM((8, 32, 256), BF16),
            pltpu.VMEM((7, 32, 256), BF16),
            pltpu.VMEM((32, 1, 256), F32),
            pltpu.VMEM((31, 1, 256), F32),
            pltpu.SemaphoreType.DMA((3,)),
            pltpu.SemaphoreType.DMA((2, 4)),
            pltpu.SemaphoreType.DMA((2, 31)),
            pltpu.SemaphoreType.DMA((2, 7)),
            pltpu.SemaphoreType.DMA((2, 1)),
            pltpu.SemaphoreType.DMA((2, 1)),
            pltpu.SemaphoreType.DMA((2, 7)),
            pltpu.SemaphoreType.DMA((2, 31)),
        ],
        compiler_params=pltpu.CompilerParams(
            collective_id=0, has_side_effects=True, vmem_limit_bytes=48 * 2**20
        ),
    )(act, cot, par)


def update_kernel(result, input_grad, grad, par, one, two, result_out, input_grad_out, new_par, new_one, new_two, sems):
    copies = start([
        pltpu.make_async_copy(result, result_out, sems.at[0]),
        pltpu.make_async_copy(input_grad, input_grad_out, sems.at[1]),
    ])
    scaled = grad[:, 0:SHARE] / jnp.sqrt(F32(64 * 32 * 16 * 64))
    first_moment = 0.9 * one[...] + 0.1 * scaled
    second_moment = 0.999 * two[...] + 0.001 * scaled * scaled
    change = 3.0 * (first_moment / (1.0 - 0.9**10)) / (jnp.sqrt(second_moment / (1.0 - 0.999**10)) + 1e-08)
    new_par[...] = par[...] - change
    new_one[...] = first_moment
    new_two[...] = second_moment
    for copy in copies:
        copy.wait()


def update(result, input_grad, grad, par, one, two):
    vmem, hbm = pl.BlockSpec(memory_space=pltpu.VMEM), pl.BlockSpec(memory_space=pltpu.HBM)
    planes = jax.ShapeDtypeStruct((4, 16, 4096), BF16)
    share = jax.ShapeDtypeStruct((1, SHARE), F32)
    return pl.pallas_call(
        update_kernel,
        out_shape=(planes, planes) + (share,) * 3,
        in_specs=[vmem] * 6,
        out_specs=(hbm,) * 2 + (vmem,) * 3,
        scratch_shapes=[pltpu.SemaphoreType.DMA((2,))],
        compiler_params=pltpu.CompilerParams(vmem_limit_bytes=8 * 2**20),
    )(result, input_grad, grad, par, one, two)


def on_device(activations, cotangent, params, moment_one, moment_two):
    par, one, two = (a.reshape(1, SHARE) for a in (params, moment_one, moment_two))
    result, input_grad, grad = step(activations[0], cotangent[0], par)
    result, input_grad, new_par, new_one, new_two = update(result, input_grad, grad, par, one, two)
    return (
        result[None],
        input_grad[None],
        new_par.reshape(SHARE),
        new_one.reshape(SHARE),
        new_two.reshape(SHARE),
    )


def solution(mesh):
    field, share = P("dp", "slab", None, None), P(("slab", "dp"))
    return jax.shard_map(
        on_device,
        mesh=mesh,
        in_specs=(field, field, share, share, share),
        out_specs=(field, field, share, share, share),
        check_vma=False,
    )
```

```python
import jax
import jax.numpy as jnp
from jax import lax
from jax.experimental import pallas as pl
from jax.experimental.pallas import tpu as pltpu
from jax.sharding import PartitionSpec as P

MESH = pl.DeviceIdType.MESH
F32 = jnp.float32
BF16 = jnp.bfloat16
SHARE = 216
PLANE = 512
VMEM_MIB = 52.5


def place():
    slab, dp = lax.axis_index("slab"), lax.axis_index("dp")
    return {
        "slab": slab,
        "dp": dp,
        "x": slab % 4,
        "y": (dp // 16) * 2 + slab // 4,
        "row": slab * 4 + dp // 16,
        "z": (dp // 2) % 8,
        "core": dp % 2,
    }


def hops(d, n):
    return min(d, n - d)


XY = sorted(
    [(dx, dy) for dx in range(4) for dy in range(8) if dx or dy],
    key=lambda o: -(hops(o[0], 4) + hops(o[1], 8)),
)
X, EIGHT = (2, 1, 3), sorted(range(1, 8), key=lambda d: -hops(d, 8))


def xy_peer(me, offset):
    x, y = (me["x"] + offset[0]) % 4, (me["y"] + offset[1]) % 8
    return ((y % 2) * 4 + x, (y // 2) * 16 + me["dp"] % 16)


def x_peer(me, d):
    return xy_peer(me, (d, 0))


def y_peer(me, d):
    return xy_peer(me, (0, d))


def xy_row(me, offset):
    slab, dp = xy_peer(me, offset)
    return slab * 4 + dp // 16


def z_peer(me, d):
    return (me["slab"], (me["dp"] // 16) * 16 + ((me["z"] + d) % 8) * 2 + me["core"])


def core_peer(me):
    return (me["slab"], me["dp"] + 1 - 2 * me["core"])


def slab_peer(me, d):
    return ((me["slab"] + d) % 8, me["dp"])


def remote(src, dst, sems, index, peer):
    return pltpu.make_async_remote_copy(
        src_ref=src,
        dst_ref=dst,
        send_sem=sems.at[0, index],
        recv_sem=sems.at[1, index],
        device_id=peer,
        device_id_type=MESH,
    )


def start(copies):
    for copy in copies:
        copy.start()
    return copies


def wait_recv(copies):
    for copy in copies:
        copy.wait_recv()


def wait_send(copies):
    for copy in copies:
        copy.wait_send()


def iota(shape, axis):
    return lax.broadcasted_iota(jnp.int32, shape, axis)


def spread(field, out, p, keep=None):
    moved = pltpu.roll(field[p].astype(F32), 64, 1)
    if keep is not None:
        moved = jnp.where(keep, moved, 0.0)
    lane = iota((16, 128), 1)
    line = iota((16, 128), 0)
    base = p * PLANE if isinstance(p, int) else pl.multiple_of(p * PLANE, PLANE)
    for chunk in range(33):
        if chunk == 0:
            cells = jnp.where(lane >= 64, moved[:, 0:128], 0.0)
        elif chunk == 32:
            cells = jnp.where(lane < 64, moved[:, 0:128], 0.0)
        else:
            cells = moved[:, 128 * chunk : 128 * chunk + 128]
        above = jnp.where(line > 0, pltpu.roll(cells, 1, 0), 0.0)
        below = jnp.where(line < 15, pltpu.roll(cells, 15, 0), 0.0)
        for ky, part in enumerate((above, cells, below)):
            part = part.astype(BF16)
            if chunk < 32:
                out[pl.ds(base + 16 * chunk, 16), 256 * ky : 256 * ky + 128] = part
            if chunk > 0:
                out[pl.ds(base + 16 * (chunk - 1), 16), 256 * ky + 128 : 256 * ky + 256] = part


def turn(field, out, p):
    plane = field[p]
    stacked = jnp.concatenate([plane[:, 128 * g : 128 * g + 128] for g in range(32)], axis=0)
    out[pl.ds((p - 1) * 128, 128), :] = stacked.T


def kernel_gradient(turned, spread_cot, total, planes):
    for p in planes:
        low, high = max(0, 2 - p), min(2, 5 - p)
        first, count = p - 2 + low, high - low + 1
        term = jnp.dot(
            turned[first * 128 : (first + count) * 128, :],
            spread_cot[p * PLANE : (p + 1) * PLANE, :],
            preferred_element_type=F32,
        )
        if p == 2:
            total[...] = term
        else:
            total[low * 128 : (high + 1) * 128, :] += term


def fold(total, flat):
    for kz in range(3):
        for ky in range(3):
            at = 256 * (2 - ky)
            left = total[kz * 128 : kz * 128 + 64, at : at + 256]
            right = total[kz * 128 + 64 : kz * 128 + 128, at : at + 256]
            both = left + pltpu.roll(right, 192, 1)
            row = (kz * 3 + ky) * 3 * 64
            flat[row : row + 64, :] = both[:, 128:256]
            flat[row + 64 : row + 128, :] = pltpu.roll(both[:, 0:128], 64, 1)
            flat[row + 128 : row + 192, :] = both[:, 0:128]


def to_shares(flat, shares):
    lane = iota((32, 128), 1)
    for zh in range(2):
        source = [flat[pl.ds(27 * zh + r, 32, stride=54), :] for r in range(27)]
        for s in range(8):
            halves = [jnp.zeros((32, 128), F32), jnp.zeros((32, 128), F32)]
            for r in range(SHARE * s // 64, (SHARE * s + SHARE - 1) // 64 + 1):
                at = 64 * r - SHARE * s
                moved = pltpu.roll(source[r], at % 128, 1) if at % 128 else source[r]
                low, high = max(at, 0), min(at + 64, SHARE)
                for h in range(2):
                    begin, end = max(low - 128 * h, 0), min(high - 128 * h, 128)
                    if begin < end:
                        halves[h] = jnp.where((lane >= begin) & (lane < end), moved, halves[h])
            for h in range(2):
                shares[s % 2, zh * 4 + s // 2, :, 128 * h : 128 * h + 128] = halves[h]


def from_shares(shares, flat):
    lane = iota((32, 128), 1)
    for zh in range(2):
        source = [
            [shares[s % 2, zh * 4 + s // 2, :, 128 * h : 128 * h + 128].astype(F32) for h in range(2)]
            for s in range(8)
        ]
        for r in range(27):
            out = jnp.zeros((32, 128), F32)
            for s in range(64 * r // SHARE, (64 * r + 63) // SHARE + 1):
                shift = SHARE * s - 64 * r
                low, high = max(64 * r, SHARE * s) - SHARE * s, min(64 * r + 64, SHARE * (s + 1)) - SHARE * s
                for h in range(2):
                    begin, end = max(low, 128 * h), min(high, 128 * h + 128)
                    if begin < end:
                        by = (shift + 128 * h) % 128
                        moved = pltpu.roll(source[s][h], by, 1) if by else source[s][h]
                        out = jnp.where((lane >= begin + shift) & (lane < end + shift), moved, out)
            flat[pl.ds(27 * zh + r, 32, stride=54), :] = out


def bands(flat, forward, backward):
    zero = jnp.zeros((256, 128), BF16)
    for out in (forward, backward):
        for ky in range(3):
            out[256 * ky : 256 * ky + 256, 128:256] = zero
            out[3 * 768 + 256 * ky : 3 * 768 + 256 * ky + 256, 0:128] = zero
    for kz in range(3):
        for ky in range(3):
            row = (kz * 3 + ky) * 3 * 64
            taps = [flat[row + 64 * kx : row + 64 * kx + 64, :] for kx in range(3)]
            moved = [pltpu.roll(tap, 64, 1) for tap in taps]
            blocks = (taps[0], taps[1] + moved[0], taps[2] + moved[1], moved[2])
            ahead = jnp.concatenate(blocks, axis=0).astype(BF16)
            left = jnp.concatenate([taps[2] + moved[1], moved[2]], axis=0)
            right = jnp.concatenate([taps[0], taps[1] + moved[0]], axis=0)
            back = jnp.concatenate([left.T, right.T], axis=0).astype(BF16)
            for plane in range(2):
                lanes = slice(128 * plane, 128 * plane + 128)
                at = (kz + plane) * 768 + ky * 256
                forward[at : at + 256, lanes] = ahead
                at = (2 - kz + plane) * 768 + (2 - ky) * 256
                backward[at : at + 256, lanes] = back


def convolve(spread_field, band, out):
    for pair in range(2):
        at = pair * 2 * PLANE
        cells = jnp.concatenate([spread_field[at + j * PLANE : at + (j + 1) * PLANE, :] for j in range(4)], axis=1)
        rounded = jnp.dot(cells, band[...], preferred_element_type=F32).astype(BF16)
        for plane in range(2):
            for g in range(32):
                out[2 * pair + plane, :, 128 * g : 128 * g + 128] = rounded[
                    16 * g : 16 * g + 16, 128 * plane : 128 * plane + 128
                ]


def step_kernel(
    act, cot, par, one, two, result, input_grad, new_par, new_one, new_two,
    act_pad, cot_pad, share, row, rows, wide,
    a3, b3, turned, total, flat, forward, backward,
    shares, got, mine, sent, parts, terms, term_parts,
    local, hs, gx, gy, gz, gc, rc, rz, rx,
):
    me = place()
    barrier = pltpu.get_barrier_semaphore()
    peers = (
        [z_peer(me, d) for d in EIGHT]
        + [y_peer(me, d) for d in EIGHT]
        + [x_peer(me, d) for d in X]
        + [slab_peer(me, 1), slab_peer(me, 7), core_peer(me)]
    )
    loads = start([
        pltpu.make_async_copy(par, share.at[0], local.at[0]),
        pltpu.make_async_copy(cot, cot_pad.at[pl.ds(1, 4)], local.at[1]),
        pltpu.make_async_copy(act, act_pad.at[pl.ds(1, 4)], local.at[2]),
        pltpu.make_async_copy(one, share.at[1], local.at[3]),
        pltpu.make_async_copy(two, share.at[2], local.at[4]),
    ])
    for peer in peers:
        pl.semaphore_signal(barrier, inc=1, device_id=peer, device_id_type=MESH)
    row[...] = jnp.zeros_like(row)
    loads[0].wait()
    row[0, :, 0:SHARE] = share[0]
    rows[me["y"], me["x"]] = row[0]
    pl.semaphore_wait(barrier, len(peers))

    cot_halo = start([
        remote(cot.at[3], cot_pad.at[0], hs, 0, slab_peer(me, 1)),
        remote(cot.at[0], cot_pad.at[5], hs, 1, slab_peer(me, 7)),
    ])
    own = rows.at[me["y"], me["x"]]
    gather_x = start([remote(row.at[0], own, gx, k, x_peer(me, d)) for k, d in enumerate(X)])

    def inner(pad, out):
        @pl.loop(1, 5)
        def _(p):
            spread(pad, out, p)

    def edges(pad, out):
        @pl.loop(0, 2)
        def _(k):
            spread(pad, out, 5 * k, me["slab"] != 7 * k)

    loads[1].wait()
    inner(cot_pad, b3)
    loads[2].wait()
    for p in range(1, 5):
        turn(act_pad, turned, p)
    kernel_gradient(turned, b3, total, (2, 3, 1, 4))
    wait_recv(gather_x)
    four = rows.at[me["y"]]
    gather_y = start([remote(four, four, gy, k, y_peer(me, d)) for k, d in enumerate(EIGHT)])
    inner(act_pad, a3)
    loads[3].wait()
    loads[4].wait()

    wait_recv(cot_halo)
    act_halo = start([
        remote(act.at[3], act_pad.at[0], hs, 2, slab_peer(me, 1)),
        remote(act.at[0], act_pad.at[5], hs, 3, slab_peer(me, 7)),
    ])
    edges(cot_pad, b3)
    kernel_gradient(turned, b3, total, (0, 5))
    fold(total, flat)
    to_shares(flat, shares)
    sum_core = start([remote(shares.at[1 - me["core"]], got, rc, 0, core_peer(me))])

    wait_recv(gather_y)
    wide[me["core"], me["z"]] = jnp.concatenate(
        [rows[(k % 4) * 2 + k // 16, (k // 4) % 4] for k in range(32)], axis=0
    ).astype(BF16)
    block = wide.at[me["core"], me["z"]]
    gather_z = start([remote(block, block, gz, k, z_peer(me, d)) for k, d in enumerate(EIGHT)])

    wait_recv(sum_core)
    for k in range(8):
        both = shares[me["core"], k] + got[k]
        mine[k] = both
        sent[k] = both.astype(BF16)
    sum_z = start([remote(sent.at[(me["z"] + d) % 8], parts.at[k], rz, k, z_peer(me, d)) for k, d in enumerate(EIGHT)])
    wait_recv(act_halo)
    edges(act_pad, a3)

    wait_recv(gather_z)
    half = wide.at[me["core"]]
    gather_core = start([remote(half, half, gc, 0, core_peer(me))])
    wait_recv(gather_core)
    from_shares(wide, flat)
    bands(flat, forward, backward)

    wait_recv(sum_z)
    summed = mine[me["z"]]
    for k in range(7):
        summed = summed + parts[k].astype(F32)
    for k in range(32):
        terms[k] = summed[k : k + 1, :]
    sum_xy = start([
        remote(terms.at[xy_row(me, o)], term_parts.at[k], rx, k, xy_peer(me, o)) for k, o in enumerate(XY)
    ])

    convolve(a3, forward, result)
    convolve(b3, backward, input_grad)

    wait_recv(sum_xy)
    summed = terms[me["row"]]
    for k in range(31):
        summed = summed + term_parts[k]
    scaled = summed[:, 0:SHARE] / jnp.sqrt(F32(64 * 32 * 16 * 64))
    first_moment = 0.9 * share[1] + 0.1 * scaled
    second_moment = 0.999 * share[2] + 0.001 * scaled * scaled
    change = 3.0 * (first_moment / (1.0 - 0.9**10)) / (jnp.sqrt(second_moment / (1.0 - 0.999**10)) + 1e-08)
    new_par[...] = share[0] - change
    new_one[...] = first_moment
    new_two[...] = second_moment
    wait_send(cot_halo + gather_x + gather_y + act_halo + gather_z + sum_core + sum_z + gather_core + sum_xy)


def step(act, cot, par, one, two):
    vmem, hbm = pl.BlockSpec(memory_space=pltpu.VMEM), pl.BlockSpec(memory_space=pltpu.HBM)
    planes = jax.ShapeDtypeStruct((4, 16, 4096), BF16)
    share = jax.ShapeDtypeStruct((1, SHARE), F32)
    return pl.pallas_call(
        step_kernel,
        out_shape=(planes, planes) + (share,) * 3,
        in_specs=[hbm] * 5,
        out_specs=(vmem,) * 5,
        scratch_shapes=[
            pltpu.VMEM((6, 16, 4096), BF16),
            pltpu.VMEM((6, 16, 4096), BF16),
            pltpu.VMEM((3, 1, SHARE), F32),
            pltpu.VMEM((1, 1, 256), F32),
            pltpu.VMEM((8, 4, 1, 256), F32),
            pltpu.VMEM((2, 8, 32, 256), BF16),
            pltpu.VMEM((6 * PLANE, 768), BF16),
            pltpu.VMEM((6 * PLANE, 768), BF16),
            pltpu.VMEM((512, 512), BF16),
            pltpu.VMEM((384, 768), F32),
            pltpu.VMEM((1728, 128), F32),
            pltpu.VMEM((3072, 256), BF16),
            pltpu.VMEM((3072, 256), BF16),
            pltpu.VMEM((2, 8, 32, 256), F32),
            pltpu.VMEM((8, 32, 256), F32),
            pltpu.VMEM((8, 32, 256), F32),
            pltpu.VMEM((8, 32, 256), BF16),
            pltpu.VMEM((7, 32, 256), BF16),
            pltpu.VMEM((32, 1, 256), F32),
            pltpu.VMEM((31, 1, 256), F32),
            pltpu.SemaphoreType.DMA((5,)),
            pltpu.SemaphoreType.DMA((2, 4)),
            pltpu.SemaphoreType.DMA((2, 3)),
            pltpu.SemaphoreType.DMA((2, 7)),
            pltpu.SemaphoreType.DMA((2, 7)),
            pltpu.SemaphoreType.DMA((2, 1)),
            pltpu.SemaphoreType.DMA((2, 1)),
            pltpu.SemaphoreType.DMA((2, 7)),
            pltpu.SemaphoreType.DMA((2, 31)),
        ],
        compiler_params=pltpu.CompilerParams(
            collective_id=0, has_side_effects=True, vmem_limit_bytes=int(VMEM_MIB * 2**20)
        ),
    )(act, cot, par, one, two)


def place_kernel(*refs):
    sems = refs[-1]
    copies = start([pltpu.make_async_copy(refs[k], refs[k + 5], sems.at[k]) for k in range(5)])
    for copy in copies:
        copy.wait()


def place_outputs(*arrays):
    hbm = pl.BlockSpec(memory_space=pltpu.HBM)
    return pl.pallas_call(
        place_kernel,
        out_shape=tuple(jax.ShapeDtypeStruct(a.shape, a.dtype) for a in arrays),
        in_specs=[hbm] * 5,
        out_specs=(hbm,) * 5,
        scratch_shapes=[pltpu.SemaphoreType.DMA((5,))],
        compiler_params=pltpu.CompilerParams(vmem_limit_bytes=8 * 2**20),
    )(*arrays)


def on_device(activations, cotangent, params, moment_one, moment_two):
    par, one, two = (a.reshape(1, SHARE) for a in (params, moment_one, moment_two))
    outputs = step(activations[0], cotangent[0], par, one, two)
    result, input_grad, new_par, new_one, new_two = place_outputs(*outputs)
    return (
        result[None],
        input_grad[None],
        new_par.reshape(SHARE),
        new_one.reshape(SHARE),
        new_two.reshape(SHARE),
    )


def solution(mesh):
    field, share = P("dp", "slab", None, None), P(("slab", "dp"))
    return jax.shard_map(
        on_device,
        mesh=mesh,
        in_specs=(field, field, share, share, share),
        out_specs=(field, field, share, share, share),
        check_vma=False,
    )
```

```python
import jax
import jax.numpy as jnp
from jax import lax
from jax.experimental import pallas as pl
from jax.experimental.pallas import tpu as pltpu
from jax.sharding import PartitionSpec as P

MESH = pl.DeviceIdType.MESH
F32 = jnp.float32
BF16 = jnp.bfloat16
SHARE = 216
PLANE = 512
VMEM_MIB = 52.5


def place():
    slab, dp = lax.axis_index("slab"), lax.axis_index("dp")
    return {
        "slab": slab,
        "dp": dp,
        "x": slab % 4,
        "y": (dp // 16) * 2 + slab // 4,
        "row": slab * 4 + dp // 16,
        "z": (dp // 2) % 8,
        "z_row": ((dp // 2) % 4) * 2 + (dp // 8) % 2,
        "core": dp % 2,
    }


def hops(d, n):
    return min(d, n - d)


XY = sorted(
    [(dx, dy) for dx in range(4) for dy in range(8) if dx or dy],
    key=lambda o: -(hops(o[0], 4) + hops(o[1], 8)),
)
X, EIGHT = (2, 1, 3), sorted(range(1, 8), key=lambda d: -hops(d, 8))


def xy_peer(me, offset):
    x, y = (me["x"] + offset[0]) % 4, (me["y"] + offset[1]) % 8
    return ((y % 2) * 4 + x, (y // 2) * 16 + me["dp"] % 16)


def x_peer(me, d):
    return xy_peer(me, (d, 0))


def y_peer(me, d):
    return xy_peer(me, (0, d))


def xy_row(me, offset):
    slab, dp = xy_peer(me, offset)
    return slab * 4 + dp // 16


def z_peer(me, d):
    return (me["slab"], (me["dp"] // 16) * 16 + ((me["z"] + d) % 8) * 2 + me["core"])


def core_peer(me):
    return (me["slab"], me["dp"] + 1 - 2 * me["core"])


def slab_peer(me, d):
    return ((me["slab"] + d) % 8, me["dp"])


def remote(src, dst, sems, index, peer):
    return pltpu.make_async_remote_copy(
        src_ref=src,
        dst_ref=dst,
        send_sem=sems.at[0, index],
        recv_sem=sems.at[1, index],
        device_id=peer,
        device_id_type=MESH,
    )


def start(copies):
    for copy in copies:
        copy.start()
    return copies


def wait_recv(copies):
    for copy in copies:
        copy.wait_recv()


def wait_send(copies):
    for copy in copies:
        copy.wait_send()


def iota(shape, axis):
    return lax.broadcasted_iota(jnp.int32, shape, axis)


def spread(field, out, p, keep=None):
    moved = pltpu.roll(field[p].astype(F32), 64, 1)
    if keep is not None:
        moved = jnp.where(keep, moved, 0.0)
    lane = iota((16, 128), 1)
    line = iota((16, 128), 0)
    base = p * PLANE if isinstance(p, int) else pl.multiple_of(p * PLANE, PLANE)
    for chunk in range(33):
        if chunk == 0:
            cells = jnp.where(lane >= 64, moved[:, 0:128], 0.0)
        elif chunk == 32:
            cells = jnp.where(lane < 64, moved[:, 0:128], 0.0)
        else:
            cells = moved[:, 128 * chunk : 128 * chunk + 128]
        above = jnp.where(line > 0, pltpu.roll(cells, 1, 0), 0.0)
        below = jnp.where(line < 15, pltpu.roll(cells, 15, 0), 0.0)
        for ky, part in enumerate((above, cells, below)):
            part = part.astype(BF16)
            if chunk < 32:
                out[pl.ds(base + 16 * chunk, 16), 256 * ky : 256 * ky + 128] = part
            if chunk > 0:
                out[pl.ds(base + 16 * (chunk - 1), 16), 256 * ky + 128 : 256 * ky + 256] = part


def turn(field, out, p):
    plane = field[p]
    stacked = jnp.concatenate([plane[:, 128 * g : 128 * g + 128] for g in range(32)], axis=0)
    out[pl.ds((p - 1) * 128, 128), :] = stacked.T


def kernel_gradient(turned, spread_cot, total, planes):
    for p in planes:
        low, high = max(0, 2 - p), min(2, 5 - p)
        first, count = p - 2 + low, high - low + 1
        term = jnp.dot(
            turned[first * 128 : (first + count) * 128, :],
            spread_cot[p * PLANE : (p + 1) * PLANE, :],
            preferred_element_type=F32,
        )
        if p == 2:
            total[...] = term
        else:
            total[low * 128 : (high + 1) * 128, :] += term


def fold(total, flat, planes):
    for kz in planes:
        for ky in range(3):
            at = 256 * (2 - ky)
            left = total[kz * 128 : kz * 128 + 64, at : at + 256]
            right = total[kz * 128 + 64 : kz * 128 + 128, at : at + 256]
            both = left + pltpu.roll(right, 192, 1)
            row = (kz * 3 + ky) * 3 * 64
            flat[row : row + 64, :] = both[:, 128:256]
            flat[row + 64 : row + 128, :] = pltpu.roll(both[:, 0:128], 64, 1)
            flat[row + 128 : row + 192, :] = both[:, 0:128]


def to_shares(flat, shares):
    lane = iota((32, 128), 1)
    for zh in range(2):
        source = [flat[pl.ds(27 * zh + r, 32, stride=54), :] for r in range(27)]
        for s in range(8):
            halves = [jnp.zeros((32, 128), F32), jnp.zeros((32, 128), F32)]
            for r in range(SHARE * s // 64, (SHARE * s + SHARE - 1) // 64 + 1):
                at = 64 * r - SHARE * s
                moved = pltpu.roll(source[r], at % 128, 1) if at % 128 else source[r]
                low, high = max(at, 0), min(at + 64, SHARE)
                for h in range(2):
                    begin, end = max(low - 128 * h, 0), min(high - 128 * h, 128)
                    if begin < end:
                        halves[h] = jnp.where((lane >= begin) & (lane < end), moved, halves[h])
            for h in range(2):
                shares[s % 2, zh * 4 + s // 2, :, 128 * h : 128 * h + 128] = halves[h]


def from_shares(shares, flat):
    lane = iota((64, 128), 1)
    source = []
    for s in range(8):
        rows = [shares[s % 2, y].astype(F32)[8 * (s // 2) : 8 * (s // 2) + 8, :] for y in range(8)]
        whole = jnp.concatenate(rows, axis=0)
        source.append([whole[:, 0:128], whole[:, 128:256]])
    for r in range(27):
        out = jnp.zeros((64, 128), F32)
        for s in range(64 * r // SHARE, (64 * r + 63) // SHARE + 1):
            shift = SHARE * s - 64 * r
            low, high = max(64 * r, SHARE * s) - SHARE * s, min(64 * r + 64, SHARE * (s + 1)) - SHARE * s
            for h in range(2):
                begin, end = max(low, 128 * h), min(high, 128 * h + 128)
                if begin < end:
                    by = (shift + 128 * h) % 128
                    moved = pltpu.roll(source[s][h], by, 1) if by else source[s][h]
                    out = jnp.where((lane >= begin + shift) & (lane < end + shift), moved, out)
        for k in range(16):
            y, zh = k // 2, k % 2
            first = 54 * ((y % 2) * 16 + y // 2) + 27 * zh + r
            flat[pl.ds(first, 4, stride=216), :] = out[4 * k : 4 * k + 4, :]


def bands(flat, forward, backward):
    zero = jnp.zeros((256, 128), BF16)
    for out in (forward, backward):
        for ky in range(3):
            out[256 * ky : 256 * ky + 256, 128:256] = zero
            out[3 * 768 + 256 * ky : 3 * 768 + 256 * ky + 256, 0:128] = zero
    for kz in range(3):
        for ky in range(3):
            row = (kz * 3 + ky) * 3 * 64
            taps = [flat[row + 64 * kx : row + 64 * kx + 64, :] for kx in range(3)]
            moved = [pltpu.roll(tap, 64, 1) for tap in taps]
            blocks = (taps[0], taps[1] + moved[0], taps[2] + moved[1], moved[2])
            ahead = jnp.concatenate(blocks, axis=0).astype(BF16)
            left = jnp.concatenate([taps[2] + moved[1], moved[2]], axis=0)
            right = jnp.concatenate([taps[0], taps[1] + moved[0]], axis=0)
            back = jnp.concatenate([left.T, right.T], axis=0).astype(BF16)
            for plane in range(2):
                lanes = slice(128 * plane, 128 * plane + 128)
                at = (kz + plane) * 768 + ky * 256
                forward[at : at + 256, lanes] = ahead
                at = (2 - kz + plane) * 768 + (2 - ky) * 256
                backward[at : at + 256, lanes] = back


def convolve(spread_field, band, out):
    for pair in range(2):
        at = pair * 2 * PLANE
        cells = jnp.concatenate([spread_field[at + j * PLANE : at + (j + 1) * PLANE, :] for j in range(4)], axis=1)
        rounded = jnp.dot(cells, band[...], preferred_element_type=F32).astype(BF16)
        for plane in range(2):
            for g in range(32):
                out[2 * pair + plane, :, 128 * g : 128 * g + 128] = rounded[
                    16 * g : 16 * g + 16, 128 * plane : 128 * plane + 128
                ]


def step_kernel(
    act, cot, par, one, two, result, input_grad, new_par, new_one, new_two,
    act_pad, cot_pad, share, row, rows, wide,
    a3, b3, turned, total, flat, forward, backward,
    shares, got, mine, sent, parts, terms, term_parts,
    local, come, hs, gx, gy, gz, gc, rc, rz, rx,
):
    me = place()
    barrier = pltpu.get_barrier_semaphore()
    peers = (
        [slab_peer(me, 1), slab_peer(me, 7)]
        + [x_peer(me, d) for d in X]
        + [z_peer(me, d) for d in (2, 6, 1, 7)]
        + [y_peer(me, d) for d in (2, 6, 1, 7)]
        + [core_peer(me)]
    )
    loads = start([
        pltpu.make_async_copy(par, share.at[0], local.at[0]),
        pltpu.make_async_copy(cot, cot_pad.at[pl.ds(1, 4)], local.at[1]),
        pltpu.make_async_copy(act, act_pad.at[pl.ds(1, 4)], local.at[2]),
        pltpu.make_async_copy(one, share.at[1], local.at[3]),
        pltpu.make_async_copy(two, share.at[2], local.at[4]),
    ])
    for peer in peers:
        pl.semaphore_signal(barrier, inc=1, device_id=peer, device_id_type=MESH)

    def greet(axis):
        for d in (2, 6):
            peer = (y_peer, z_peer)[axis](me, d)
            pl.semaphore_signal(come.at[axis], inc=1, device_id=peer, device_id_type=MESH)

    def greeted(axis):
        pl.semaphore_wait(come.at[axis], 2)

    def inner(pad, out):
        @pl.loop(1, 5)
        def _(p):
            spread(pad, out, p)

    def edges(pad, out):
        @pl.loop(0, 2)
        def _(k):
            spread(pad, out, 5 * k, me["slab"] != 7 * k)

    row[...] = jnp.zeros_like(row)
    loads[0].wait()
    row[0, :, 0:SHARE] = share[0]
    rows[me["z_row"], me["x"]] = row[0]
    loads[1].wait()
    inner(cot_pad, b3)
    loads[2].wait()
    for p in range(1, 5):
        turn(act_pad, turned, p)
    pl.semaphore_wait(barrier, len(peers))

    greet(1)
    cot_halo = start([
        remote(cot_pad.at[4], cot_pad.at[0], hs, 0, slab_peer(me, 1)),
        remote(cot_pad.at[1], cot_pad.at[5], hs, 1, slab_peer(me, 7)),
    ])
    own = rows.at[me["z_row"], me["x"]]
    gather_x = start([remote(row.at[0], own, gx, k, x_peer(me, d)) for k, d in enumerate(X)])
    kernel_gradient(turned, b3, total, (2, 3, 1, 4))
    fold(total, flat, (1,))
    wait_recv(gather_x)
    greet(0)
    greeted(1)
    four = rows.at[me["z_row"]]
    gather_z = start([remote(four, four, gz, k, z_peer(me, d)) for k, d in enumerate(EIGHT)])
    inner(act_pad, a3)
    loads[3].wait()
    loads[4].wait()
    wait_recv(cot_halo)
    act_halo = start([
        remote(act_pad.at[4], act_pad.at[0], hs, 2, slab_peer(me, 1)),
        remote(act_pad.at[1], act_pad.at[5], hs, 3, slab_peer(me, 7)),
    ])
    edges(cot_pad, b3)
    kernel_gradient(turned, b3, total, (0, 5))
    fold(total, flat, (0, 2))
    to_shares(flat, shares)
    sum_core = start([remote(shares.at[1 - me["core"]], got, rc, 0, core_peer(me))])
    wait_recv(sum_core)
    for k in range(8):
        both = shares[me["core"], k] + got[k]
        mine[k] = both
        sent[k] = both.astype(BF16)
    sum_z = start([
        remote(sent.at[(me["z"] + d) % 8], parts.at[k], rz, k, z_peer(me, d)) for k, d in enumerate(EIGHT)
    ])

    greeted(0)
    wait_recv(gather_z)
    wide[me["core"], me["y"]] = jnp.concatenate([rows[k // 4, k % 4] for k in range(32)], axis=0).astype(BF16)
    block = wide.at[me["core"], me["y"]]
    gather_y = start([remote(block, block, gy, k, y_peer(me, d)) for k, d in enumerate(EIGHT)])
    wait_recv(act_halo)
    edges(act_pad, a3)

    wait_recv(sum_z)
    summed = mine[me["z"]]
    for k in range(7):
        summed = summed + parts[k].astype(F32)
    for k in range(32):
        terms[k] = summed[k : k + 1, :]
    sum_xy = [remote(terms.at[xy_row(me, o)], term_parts.at[k], rx, 0, xy_peer(me, o)) for k, o in enumerate(XY)]
    start(sum_xy)
    all_xy = remote(term_parts, term_parts, rx, 0, xy_peer(me, XY[0]))
    wait_recv(gather_y)
    half = wide.at[me["core"]]
    gather_core = start([remote(half, half, gc, 0, core_peer(me))])
    wait_recv(gather_core)
    from_shares(wide, flat)
    bands(flat, forward, backward)
    convolve(a3, forward, result)
    convolve(b3, backward, input_grad)

    wait_send(cot_halo + gather_x + gather_y + act_halo + gather_z + sum_core + sum_z + gather_core)
    wait_recv([all_xy])
    summed = terms[me["row"]]
    for k in range(31):
        summed = summed + term_parts[k]
    scaled = summed[:, 0:SHARE] / jnp.sqrt(F32(64 * 32 * 16 * 64))
    first_moment = 0.9 * share[1] + 0.1 * scaled
    second_moment = 0.999 * share[2] + 0.001 * scaled * scaled
    change = 3.0 * (first_moment / (1.0 - 0.9**10)) / (jnp.sqrt(second_moment / (1.0 - 0.999**10)) + 1e-08)
    new_par[...] = share[0] - change
    new_one[...] = first_moment
    new_two[...] = second_moment
    wait_send([all_xy])


def step(act, cot, par, one, two):
    vmem, hbm = pl.BlockSpec(memory_space=pltpu.VMEM), pl.BlockSpec(memory_space=pltpu.HBM)
    planes = jax.ShapeDtypeStruct((4, 16, 4096), BF16)
    share = jax.ShapeDtypeStruct((1, SHARE), F32)
    return pl.pallas_call(
        step_kernel,
        out_shape=(planes, planes) + (share,) * 3,
        in_specs=[hbm] * 5,
        out_specs=(vmem,) * 5,
        scratch_shapes=[
            pltpu.VMEM((6, 16, 4096), BF16),
            pltpu.VMEM((6, 16, 4096), BF16),
            pltpu.VMEM((3, 1, SHARE), F32),
            pltpu.VMEM((1, 1, 256), F32),
            pltpu.VMEM((8, 4, 1, 256), F32),
            pltpu.VMEM((2, 8, 32, 256), BF16),
            pltpu.VMEM((6 * PLANE, 768), BF16),
            pltpu.VMEM((6 * PLANE, 768), BF16),
            pltpu.VMEM((512, 512), BF16),
            pltpu.VMEM((384, 768), F32),
            pltpu.VMEM((1728, 128), F32),
            pltpu.VMEM((3072, 256), BF16),
            pltpu.VMEM((3072, 256), BF16),
            pltpu.VMEM((2, 8, 32, 256), F32),
            pltpu.VMEM((8, 32, 256), F32),
            pltpu.VMEM((8, 32, 256), F32),
            pltpu.VMEM((8, 32, 256), BF16),
            pltpu.VMEM((7, 32, 256), BF16),
            pltpu.VMEM((32, 1, 256), F32),
            pltpu.VMEM((31, 1, 256), F32),
            pltpu.SemaphoreType.DMA((5,)),
            pltpu.SemaphoreType.REGULAR((2,)),
            pltpu.SemaphoreType.DMA((2, 4)),
            pltpu.SemaphoreType.DMA((2, 3)),
            pltpu.SemaphoreType.DMA((2, 7)),
            pltpu.SemaphoreType.DMA((2, 7)),
            pltpu.SemaphoreType.DMA((2, 1)),
            pltpu.SemaphoreType.DMA((2, 1)),
            pltpu.SemaphoreType.DMA((2, 7)),
            pltpu.SemaphoreType.DMA((2, 1)),
        ],
        compiler_params=pltpu.CompilerParams(
            collective_id=0, has_side_effects=True, vmem_limit_bytes=int(VMEM_MIB * 2**20)
        ),
    )(act, cot, par, one, two)


def place_kernel(*refs):
    sems = refs[-1]
    copies = start([pltpu.make_async_copy(refs[k], refs[k + 5], sems.at[k]) for k in range(5)])
    for copy in copies:
        copy.wait()


def place_outputs(*arrays):
    hbm = pl.BlockSpec(memory_space=pltpu.HBM)
    return pl.pallas_call(
        place_kernel,
        out_shape=tuple(jax.ShapeDtypeStruct(a.shape, a.dtype) for a in arrays),
        in_specs=[hbm] * 5,
        out_specs=(hbm,) * 5,
        scratch_shapes=[pltpu.SemaphoreType.DMA((5,))],
        compiler_params=pltpu.CompilerParams(vmem_limit_bytes=8 * 2**20),
    )(*arrays)


def on_device(activations, cotangent, params, moment_one, moment_two):
    par, one, two = (a.reshape(1, SHARE) for a in (params, moment_one, moment_two))
    outputs = step(activations[0], cotangent[0], par, one, two)
    result, input_grad, new_par, new_one, new_two = place_outputs(*outputs)
    return (
        result[None],
        input_grad[None],
        new_par.reshape(SHARE),
        new_one.reshape(SHARE),
        new_two.reshape(SHARE),
    )


def solution(mesh):
    field, share = P("dp", "slab", None, None), P(("slab", "dp"))
    return jax.shard_map(
        on_device,
        mesh=mesh,
        in_specs=(field, field, share, share, share),
        out_specs=(field, field, share, share, share),
        check_vma=False,
    )
```

```python
import jax
import jax.numpy as jnp
from jax import lax
from jax.experimental import pallas as pl
from jax.experimental.pallas import tpu as pltpu
from jax.sharding import PartitionSpec as P

MESH = pl.DeviceIdType.MESH
F32 = jnp.float32
BF16 = jnp.bfloat16
SHARE = 216
PLANE = 512
VMEM_MIB = 52.5


def place():
    slab, dp = lax.axis_index("slab"), lax.axis_index("dp")
    return {
        "slab": slab,
        "dp": dp,
        "x": slab % 4,
        "y": (dp // 16) * 2 + slab // 4,
        "row": slab * 4 + dp // 16,
        "z": (dp // 2) % 8,
        "z_row": ((dp // 2) % 4) * 2 + (dp // 8) % 2,
        "core": dp % 2,
    }


def hops(d, n):
    return min(d, n - d)


XY = sorted(
    [(dx, dy) for dx in range(4) for dy in range(8) if dx or dy],
    key=lambda o: -(hops(o[0], 4) + hops(o[1], 8)),
)
X, EIGHT = (2, 1, 3), sorted(range(1, 8), key=lambda d: -hops(d, 8))


def xy_peer(me, offset):
    x, y = (me["x"] + offset[0]) % 4, (me["y"] + offset[1]) % 8
    return ((y % 2) * 4 + x, (y // 2) * 16 + me["dp"] % 16)


def x_peer(me, d):
    return xy_peer(me, (d, 0))


def y_peer(me, d):
    return xy_peer(me, (0, d))


def xy_row(me, offset):
    slab, dp = xy_peer(me, offset)
    return slab * 4 + dp // 16


def z_peer(me, d):
    return (me["slab"], (me["dp"] // 16) * 16 + ((me["z"] + d) % 8) * 2 + me["core"])


def core_peer(me):
    return (me["slab"], me["dp"] + 1 - 2 * me["core"])


def slab_peer(me, d):
    return ((me["slab"] + d) % 8, me["dp"])


def remote(src, dst, sems, index, peer):
    return pltpu.make_async_remote_copy(
        src_ref=src,
        dst_ref=dst,
        send_sem=sems.at[0, index],
        recv_sem=sems.at[1, index],
        device_id=peer,
        device_id_type=MESH,
    )


def start(copies):
    for copy in copies:
        copy.start()
    return copies


def wait_recv(copies):
    for copy in copies:
        copy.wait_recv()


def wait_send(copies):
    for copy in copies:
        copy.wait_send()


def iota(shape, axis):
    return lax.broadcasted_iota(jnp.int32, shape, axis)


def spread(field, out, p, keep=None):
    moved = pltpu.roll(field[p].astype(F32), 64, 1)
    if keep is not None:
        moved = jnp.where(keep, moved, 0.0)
    lane = iota((16, 128), 1)
    line = iota((16, 128), 0)
    base = p * PLANE if isinstance(p, int) else pl.multiple_of(p * PLANE, PLANE)
    for chunk in range(33):
        if chunk == 0:
            cells = jnp.where(lane >= 64, moved[:, 0:128], 0.0)
        elif chunk == 32:
            cells = jnp.where(lane < 64, moved[:, 0:128], 0.0)
        else:
            cells = moved[:, 128 * chunk : 128 * chunk + 128]
        above = jnp.where(line > 0, pltpu.roll(cells, 1, 0), 0.0)
        below = jnp.where(line < 15, pltpu.roll(cells, 15, 0), 0.0)
        for ky, part in enumerate((above, cells, below)):
            part = part.astype(BF16)
            if chunk < 32:
                out[pl.ds(base + 16 * chunk, 16), 256 * ky : 256 * ky + 128] = part
            if chunk > 0:
                out[pl.ds(base + 16 * (chunk - 1), 16), 256 * ky + 128 : 256 * ky + 256] = part


def turn(field, out, p):
    plane = field[p]
    stacked = jnp.concatenate([plane[:, 128 * g : 128 * g + 128] for g in range(32)], axis=0)
    out[pl.ds((p - 1) * 128, 128), :] = stacked.T


def kernel_gradient(turned, spread_cot, total, planes):
    for p in planes:
        low, high = max(0, 2 - p), min(2, 5 - p)
        first, count = p - 2 + low, high - low + 1
        term = jnp.dot(
            turned[first * 128 : (first + count) * 128, :],
            spread_cot[p * PLANE : (p + 1) * PLANE, :],
            preferred_element_type=F32,
        )
        if p == 2:
            total[...] = term
        else:
            total[low * 128 : (high + 1) * 128, :] += term


def fold(total, flat, planes):
    for kz in planes:
        for ky in range(3):
            at = 256 * (2 - ky)
            left = total[kz * 128 : kz * 128 + 64, at : at + 256]
            right = total[kz * 128 + 64 : kz * 128 + 128, at : at + 256]
            both = left + pltpu.roll(right, 192, 1)
            row = (kz * 3 + ky) * 3 * 64
            flat[row : row + 64, :] = both[:, 128:256]
            flat[row + 64 : row + 128, :] = pltpu.roll(both[:, 0:128], 64, 1)
            flat[row + 128 : row + 192, :] = both[:, 0:128]


def to_shares(flat, shares, zh):
    lane = iota((32, 128), 1)
    source = [flat[pl.ds(27 * zh + r, 32, stride=54), :] for r in range(27)]
    for s in range(8):
        halves = [jnp.zeros((32, 128), F32), jnp.zeros((32, 128), F32)]
        for r in range(SHARE * s // 64, (SHARE * s + SHARE - 1) // 64 + 1):
            at = 64 * r - SHARE * s
            moved = pltpu.roll(source[r], at % 128, 1) if at % 128 else source[r]
            low, high = max(at, 0), min(at + 64, SHARE)
            for h in range(2):
                begin, end = max(low - 128 * h, 0), min(high - 128 * h, 128)
                if begin < end:
                    halves[h] = jnp.where((lane >= begin) & (lane < end), moved, halves[h])
        for h in range(2):
            shares[s % 2, zh * 4 + s // 2, :, 128 * h : 128 * h + 128] = halves[h]


def from_shares(shares, flat):
    lane = iota((64, 128), 1)
    source = []
    for s in range(8):
        rows = [shares[s % 2, y].astype(F32)[8 * (s // 2) : 8 * (s // 2) + 8, :] for y in range(8)]
        whole = jnp.concatenate(rows, axis=0)
        source.append([whole[:, 0:128], whole[:, 128:256]])
    for r in range(27):
        out = jnp.zeros((64, 128), F32)
        for s in range(64 * r // SHARE, (64 * r + 63) // SHARE + 1):
            shift = SHARE * s - 64 * r
            low, high = max(64 * r, SHARE * s) - SHARE * s, min(64 * r + 64, SHARE * (s + 1)) - SHARE * s
            for h in range(2):
                begin, end = max(low, 128 * h), min(high, 128 * h + 128)
                if begin < end:
                    by = (shift + 128 * h) % 128
                    moved = pltpu.roll(source[s][h], by, 1) if by else source[s][h]
                    out = jnp.where((lane >= begin + shift) & (lane < end + shift), moved, out)
        for k in range(16):
            y, zh = k // 2, k % 2
            first = 54 * ((y % 2) * 16 + y // 2) + 27 * zh + r
            flat[pl.ds(first, 4, stride=216), :] = out[4 * k : 4 * k + 4, :]


def bands(flat, forward, backward):
    zero = jnp.zeros((256, 128), BF16)
    for out in (forward, backward):
        for ky in range(3):
            out[256 * ky : 256 * ky + 256, 128:256] = zero
            out[3 * 768 + 256 * ky : 3 * 768 + 256 * ky + 256, 0:128] = zero
    for kz in range(3):
        for ky in range(3):
            row = (kz * 3 + ky) * 3 * 64
            taps = [flat[row + 64 * kx : row + 64 * kx + 64, :] for kx in range(3)]
            moved = [pltpu.roll(tap, 64, 1) for tap in taps]
            blocks = (taps[0], taps[1] + moved[0], taps[2] + moved[1], moved[2])
            ahead = jnp.concatenate(blocks, axis=0).astype(BF16)
            left = jnp.concatenate([taps[2] + moved[1], moved[2]], axis=0)
            right = jnp.concatenate([taps[0], taps[1] + moved[0]], axis=0)
            back = jnp.concatenate([left.T, right.T], axis=0).astype(BF16)
            for plane in range(2):
                lanes = slice(128 * plane, 128 * plane + 128)
                at = (kz + plane) * 768 + ky * 256
                forward[at : at + 256, lanes] = ahead
                at = (2 - kz + plane) * 768 + (2 - ky) * 256
                backward[at : at + 256, lanes] = back


def convolve(spread_field, band, out):
    for pair in range(2):
        at = pair * 2 * PLANE
        cells = jnp.concatenate([spread_field[at + j * PLANE : at + (j + 1) * PLANE, :] for j in range(4)], axis=1)
        rounded = jnp.dot(cells, band[...], preferred_element_type=F32).astype(BF16)
        for plane in range(2):
            for g in range(32):
                out[2 * pair + plane, :, 128 * g : 128 * g + 128] = rounded[
                    16 * g : 16 * g + 16, 128 * plane : 128 * plane + 128
                ]


def step_kernel(
    act, cot, par, one, two, result, input_grad, new_par, new_one, new_two,
    act_pad, cot_pad, share, row, rows, wide,
    a3, b3, turned, total, flat, forward, backward,
    shares, got, mine, sent, parts, terms, term_parts,
    local, come, hs, gx, gy, gz, gc, rc, rz, rx,
):
    me = place()
    barrier = pltpu.get_barrier_semaphore()
    peers = (
        [slab_peer(me, 1), slab_peer(me, 7)]
        + [x_peer(me, d) for d in X]
        + [z_peer(me, d) for d in (2, 6, 1, 7)]
        + [y_peer(me, d) for d in (2, 6, 1, 7)]
        + [core_peer(me)]
    )
    loads = start([
        pltpu.make_async_copy(par, share.at[0], local.at[0]),
        pltpu.make_async_copy(cot, cot_pad.at[pl.ds(1, 4)], local.at[1]),
        pltpu.make_async_copy(act, act_pad.at[pl.ds(1, 4)], local.at[2]),
        pltpu.make_async_copy(one, share.at[1], local.at[3]),
        pltpu.make_async_copy(two, share.at[2], local.at[4]),
    ])
    for peer in peers:
        pl.semaphore_signal(barrier, inc=1, device_id=peer, device_id_type=MESH)

    def greet(axis):
        for d in (2, 6):
            peer = (y_peer, z_peer)[axis](me, d)
            pl.semaphore_signal(come.at[axis], inc=1, device_id=peer, device_id_type=MESH)

    def greeted(axis):
        pl.semaphore_wait(come.at[axis], 2)

    def inner(pad, out):
        @pl.loop(1, 5)
        def _(p):
            spread(pad, out, p)

    def edges(pad, out):
        @pl.loop(0, 2)
        def _(k):
            spread(pad, out, 5 * k, me["slab"] != 7 * k)

    row[...] = jnp.zeros_like(row)
    loads[0].wait()
    row[0, :, 0:SHARE] = share[0]
    rows[me["z_row"], me["x"]] = row[0]
    loads[1].wait()
    inner(cot_pad, b3)
    loads[2].wait()
    for p in range(1, 5):
        turn(act_pad, turned, p)
    pl.semaphore_wait(barrier, len(peers))

    own = rows.at[me["z_row"], me["x"]]
    gather_x = start([remote(row.at[0], own, gx, k, x_peer(me, d)) for k, d in enumerate(X)])
    greet(1)
    cot_halo = start([
        remote(cot_pad.at[4], cot_pad.at[0], hs, 0, slab_peer(me, 1)),
        remote(cot_pad.at[1], cot_pad.at[5], hs, 1, slab_peer(me, 7)),
    ])
    kernel_gradient(turned, b3, total, (2, 3, 1, 4))
    fold(total, flat, (1,))
    wait_recv(gather_x)
    greet(0)
    greeted(1)
    four = rows.at[me["z_row"]]
    gather_z = start([remote(four, four, gz, k, z_peer(me, d)) for k, d in enumerate(EIGHT)])
    inner(act_pad, a3)
    loads[3].wait()
    loads[4].wait()
    wait_recv(cot_halo)
    act_halo = start([
        remote(act_pad.at[4], act_pad.at[0], hs, 2, slab_peer(me, 1)),
        remote(act_pad.at[1], act_pad.at[5], hs, 3, slab_peer(me, 7)),
    ])
    edges(cot_pad, b3)
    kernel_gradient(turned, b3, total, (0, 5))
    fold(total, flat, (0, 2))
    sum_core = []
    for zh in range(2):
        to_shares(flat, shares, zh)
        half = pl.ds(4 * zh, 4)
        sum_core += start([remote(shares.at[1 - me["core"], half], got.at[half], rc, zh, core_peer(me))])
    greeted(0)
    wait_recv(gather_z)
    wide[me["core"], me["y"]] = jnp.concatenate([rows[k // 4, k % 4] for k in range(32)], axis=0).astype(BF16)
    block = wide.at[me["core"], me["y"]]
    gather_y = start([remote(block, block, gy, k, y_peer(me, d)) for k, d in enumerate(EIGHT)])
    gather_core = start([remote(block, block, gc, 7, core_peer(me))])
    for k in range(8):
        if k % 4 == 0:
            wait_recv([sum_core[k // 4]])
        both = shares[me["core"], k] + got[k]
        mine[k] = both
        sent[k] = both.astype(BF16)
    sum_z = start([
        remote(sent.at[(me["z"] + d) % 8], parts.at[k], rz, k, z_peer(me, d)) for k, d in enumerate(EIGHT)
    ])

    wait_recv(act_halo)
    edges(act_pad, a3)

    for k in reversed(range(7)):
        wait_recv([gather_y[k]])
        landed = wide.at[me["core"], (me["y"] + 8 - EIGHT[k]) % 8]
        gather_core += start([remote(landed, landed, gc, k, core_peer(me))])
    wait_recv(sum_z)
    summed = mine[me["z"]]
    for k in range(7):
        summed = summed + parts[k].astype(F32)
    for k in range(32):
        terms[k] = summed[k : k + 1, :]
    sum_xy = [remote(terms.at[xy_row(me, o)], term_parts.at[k], rx, 0, xy_peer(me, o)) for k, o in enumerate(XY)]
    start(sum_xy)
    all_xy = remote(term_parts, term_parts, rx, 0, xy_peer(me, XY[0]))
    wait_recv(gather_core)
    from_shares(wide, flat)
    bands(flat, forward, backward)
    convolve(a3, forward, result)
    convolve(b3, backward, input_grad)

    wait_send(cot_halo + gather_x + gather_y + act_halo + gather_z + sum_core + sum_z + gather_core)
    wait_recv([all_xy])
    summed = terms[me["row"]]
    for k in range(31):
        summed = summed + term_parts[k]
    scaled = summed[:, 0:SHARE] / jnp.sqrt(F32(64 * 32 * 16 * 64))
    first_moment = 0.9 * share[1] + 0.1 * scaled
    second_moment = 0.999 * share[2] + 0.001 * scaled * scaled
    change = 3.0 * (first_moment / (1.0 - 0.9**10)) / (jnp.sqrt(second_moment / (1.0 - 0.999**10)) + 1e-08)
    new_par[...] = share[0] - change
    new_one[...] = first_moment
    new_two[...] = second_moment
    wait_send([all_xy])


def step(act, cot, par, one, two):
    vmem, hbm = pl.BlockSpec(memory_space=pltpu.VMEM), pl.BlockSpec(memory_space=pltpu.HBM)
    planes = jax.ShapeDtypeStruct((4, 16, 4096), BF16)
    share = jax.ShapeDtypeStruct((1, SHARE), F32)
    return pl.pallas_call(
        step_kernel,
        out_shape=(planes, planes) + (share,) * 3,
        in_specs=[hbm] * 5,
        out_specs=(vmem,) * 5,
        scratch_shapes=[
            pltpu.VMEM((6, 16, 4096), BF16),
            pltpu.VMEM((6, 16, 4096), BF16),
            pltpu.VMEM((3, 1, SHARE), F32),
            pltpu.VMEM((1, 1, 256), F32),
            pltpu.VMEM((8, 4, 1, 256), F32),
            pltpu.VMEM((2, 8, 32, 256), BF16),
            pltpu.VMEM((6 * PLANE, 768), BF16),
            pltpu.VMEM((6 * PLANE, 768), BF16),
            pltpu.VMEM((512, 512), BF16),
            pltpu.VMEM((384, 768), F32),
            pltpu.VMEM((1728, 128), F32),
            pltpu.VMEM((3072, 256), BF16),
            pltpu.VMEM((3072, 256), BF16),
            pltpu.VMEM((2, 8, 32, 256), F32),
            pltpu.VMEM((8, 32, 256), F32),
            pltpu.VMEM((8, 32, 256), F32),
            pltpu.VMEM((8, 32, 256), BF16),
            pltpu.VMEM((7, 32, 256), BF16),
            pltpu.VMEM((32, 1, 256), F32),
            pltpu.VMEM((31, 1, 256), F32),
            pltpu.SemaphoreType.DMA((5,)),
            pltpu.SemaphoreType.REGULAR((2,)),
            pltpu.SemaphoreType.DMA((2, 4)),
            pltpu.SemaphoreType.DMA((2, 3)),
            pltpu.SemaphoreType.DMA((2, 7)),
            pltpu.SemaphoreType.DMA((2, 7)),
            pltpu.SemaphoreType.DMA((2, 8)),
            pltpu.SemaphoreType.DMA((2, 2)),
            pltpu.SemaphoreType.DMA((2, 7)),
            pltpu.SemaphoreType.DMA((2, 1)),
        ],
        compiler_params=pltpu.CompilerParams(
            collective_id=0, has_side_effects=True, vmem_limit_bytes=int(VMEM_MIB * 2**20)
        ),
    )(act, cot, par, one, two)


def place_kernel(*refs):
    sems = refs[-1]
    copies = start([pltpu.make_async_copy(refs[k], refs[k + 5], sems.at[k]) for k in range(5)])
    for copy in copies:
        copy.wait()


def place_outputs(*arrays):
    hbm = pl.BlockSpec(memory_space=pltpu.HBM)
    return pl.pallas_call(
        place_kernel,
        out_shape=tuple(jax.ShapeDtypeStruct(a.shape, a.dtype) for a in arrays),
        in_specs=[hbm] * 5,
        out_specs=(hbm,) * 5,
        scratch_shapes=[pltpu.SemaphoreType.DMA((5,))],
        compiler_params=pltpu.CompilerParams(vmem_limit_bytes=8 * 2**20),
    )(*arrays)


def on_device(activations, cotangent, params, moment_one, moment_two):
    par, one, two = (a.reshape(1, SHARE) for a in (params, moment_one, moment_two))
    outputs = step(activations[0], cotangent[0], par, one, two)
    result, input_grad, new_par, new_one, new_two = place_outputs(*outputs)
    return (
        result[None],
        input_grad[None],
        new_par.reshape(SHARE),
        new_one.reshape(SHARE),
        new_two.reshape(SHARE),
    )


def solution(mesh):
    field, share = P("dp", "slab", None, None), P(("slab", "dp"))
    return jax.shard_map(
        on_device,
        mesh=mesh,
        in_specs=(field, field, share, share, share),
        out_specs=(field, field, share, share, share),
        check_vma=False,
    )
```

```python
import jax
import jax.numpy as jnp
from jax import lax
from jax.experimental import pallas as pl
from jax.experimental.pallas import tpu as pltpu
from jax.sharding import PartitionSpec as P

MESH = pl.DeviceIdType.MESH
F32 = jnp.float32
BF16 = jnp.bfloat16
SHARE = 216
PLANE = 512
VMEM_MIB = 52.5


def place():
    slab, dp = lax.axis_index("slab"), lax.axis_index("dp")
    return {
        "slab": slab,
        "dp": dp,
        "x": slab % 4,
        "y": (dp // 16) * 2 + slab // 4,
        "row": slab * 4 + dp // 16,
        "z": (dp // 2) % 8,
        "z_row": ((dp // 2) % 4) * 2 + (dp // 8) % 2,
        "core": dp % 2,
    }


def hops(d, n):
    return min(d, n - d)


XY = sorted(
    [(dx, dy) for dx in range(4) for dy in range(8) if dx or dy],
    key=lambda o: -(hops(o[0], 4) + hops(o[1], 8)),
)
X, EIGHT = (2, 1, 3), sorted(range(1, 8), key=lambda d: -hops(d, 8))


def xy_peer(me, offset):
    x, y = (me["x"] + offset[0]) % 4, (me["y"] + offset[1]) % 8
    return ((y % 2) * 4 + x, (y // 2) * 16 + me["dp"] % 16)


def x_peer(me, d):
    return xy_peer(me, (d, 0))


def y_peer(me, d):
    return xy_peer(me, (0, d))


def xy_row(me, offset):
    slab, dp = xy_peer(me, offset)
    return slab * 4 + dp // 16


def z_peer(me, d):
    return (me["slab"], (me["dp"] // 16) * 16 + ((me["z"] + d) % 8) * 2 + me["core"])


def core_peer(me):
    return (me["slab"], me["dp"] + 1 - 2 * me["core"])


def slab_peer(me, d):
    return ((me["slab"] + d) % 8, me["dp"])


def remote(src, dst, sems, index, peer):
    return pltpu.make_async_remote_copy(
        src_ref=src,
        dst_ref=dst,
        send_sem=sems.at[0, index],
        recv_sem=sems.at[1, index],
        device_id=peer,
        device_id_type=MESH,
    )


def start(copies):
    for copy in copies:
        copy.start()
    return copies


def wait_recv(copies):
    for copy in copies:
        copy.wait_recv()


def wait_send(copies):
    for copy in copies:
        copy.wait_send()


def iota(shape, axis):
    return lax.broadcasted_iota(jnp.int32, shape, axis)


def spread(field, out, p, keep=None):
    moved = pltpu.roll(field[p].astype(F32), 64, 1)
    if keep is not None:
        moved = jnp.where(keep, moved, 0.0)
    lane = iota((16, 128), 1)
    line = iota((16, 128), 0)
    base = p * PLANE if isinstance(p, int) else pl.multiple_of(p * PLANE, PLANE)
    for chunk in range(33):
        if chunk == 0:
            cells = jnp.where(lane >= 64, moved[:, 0:128], 0.0)
        elif chunk == 32:
            cells = jnp.where(lane < 64, moved[:, 0:128], 0.0)
        else:
            cells = moved[:, 128 * chunk : 128 * chunk + 128]
        above = jnp.where(line > 0, pltpu.roll(cells, 1, 0), 0.0)
        below = jnp.where(line < 15, pltpu.roll(cells, 15, 0), 0.0)
        for ky, part in enumerate((above, cells, below)):
            part = part.astype(BF16)
            if chunk < 32:
                out[pl.ds(base + 16 * chunk, 16), 256 * ky : 256 * ky + 128] = part
            if chunk > 0:
                out[pl.ds(base + 16 * (chunk - 1), 16), 256 * ky + 128 : 256 * ky + 256] = part


def turn(field, out, p):
    plane = field[p]
    stacked = jnp.concatenate([plane[:, 128 * g : 128 * g + 128] for g in range(32)], axis=0)
    out[pl.ds((p - 1) * 128, 128), :] = stacked.T


def kernel_gradient(turned, spread_cot, total, planes):
    for p in planes:
        low, high = max(0, 2 - p), min(2, 5 - p)
        first, count = p - 2 + low, high - low + 1
        term = jnp.dot(
            turned[first * 128 : (first + count) * 128, :],
            spread_cot[p * PLANE : (p + 1) * PLANE, :],
            preferred_element_type=F32,
        )
        if p == 2:
            total[...] = term
        else:
            total[low * 128 : (high + 1) * 128, :] += term


def fold(total, flat, planes):
    for kz in planes:
        for ky in range(3):
            at = 256 * (2 - ky)
            left = total[kz * 128 : kz * 128 + 64, at : at + 256]
            right = total[kz * 128 + 64 : kz * 128 + 128, at : at + 256]
            both = left + pltpu.roll(right, 192, 1)
            row = (kz * 3 + ky) * 3 * 64
            flat[row : row + 64, :] = both[:, 128:256]
            flat[row + 64 : row + 128, :] = pltpu.roll(both[:, 0:128], 64, 1)
            flat[row + 128 : row + 192, :] = both[:, 0:128]


def to_shares(flat, shares, zh):
    lane = iota((32, 128), 1)
    source = [flat[pl.ds(27 * zh + r, 32, stride=54), :] for r in range(27)]
    for s in range(8):
        halves = [jnp.zeros((32, 128), F32), jnp.zeros((32, 128), F32)]
        for r in range(SHARE * s // 64, (SHARE * s + SHARE - 1) // 64 + 1):
            at = 64 * r - SHARE * s
            moved = pltpu.roll(source[r], at % 128, 1) if at % 128 else source[r]
            low, high = max(at, 0), min(at + 64, SHARE)
            for h in range(2):
                begin, end = max(low - 128 * h, 0), min(high - 128 * h, 128)
                if begin < end:
                    halves[h] = jnp.where((lane >= begin) & (lane < end), moved, halves[h])
        for h in range(2):
            shares[s % 2, zh * 4 + s // 2, :, 128 * h : 128 * h + 128] = halves[h]


def from_shares(shares, flat):
    lane = iota((64, 128), 1)
    source = []
    for s in range(8):
        rows = [shares[s % 2, y].astype(F32)[8 * (s // 2) : 8 * (s // 2) + 8, :] for y in range(8)]
        whole = jnp.concatenate(rows, axis=0)
        source.append([whole[:, 0:128], whole[:, 128:256]])
    for r in range(27):
        out = jnp.zeros((64, 128), F32)
        for s in range(64 * r // SHARE, (64 * r + 63) // SHARE + 1):
            shift = SHARE * s - 64 * r
            low, high = max(64 * r, SHARE * s) - SHARE * s, min(64 * r + 64, SHARE * (s + 1)) - SHARE * s
            for h in range(2):
                begin, end = max(low, 128 * h), min(high, 128 * h + 128)
                if begin < end:
                    by = (shift + 128 * h) % 128
                    moved = pltpu.roll(source[s][h], by, 1) if by else source[s][h]
                    out = jnp.where((lane >= begin + shift) & (lane < end + shift), moved, out)
        for k in range(16):
            y, zh = k // 2, k % 2
            first = 54 * ((y % 2) * 16 + y // 2) + 27 * zh + r
            flat[pl.ds(first, 4, stride=216), :] = out[4 * k : 4 * k + 4, :]


def bands(flat, forward, backward):
    zero = jnp.zeros((256, 128), BF16)
    for out in (forward, backward):
        for ky in range(3):
            out[256 * ky : 256 * ky + 256, 128:256] = zero
            out[3 * 768 + 256 * ky : 3 * 768 + 256 * ky + 256, 0:128] = zero
    for kz in range(3):
        for ky in range(3):
            row = (kz * 3 + ky) * 3 * 64
            taps = [flat[row + 64 * kx : row + 64 * kx + 64, :] for kx in range(3)]
            moved = [pltpu.roll(tap, 64, 1) for tap in taps]
            blocks = (taps[0], taps[1] + moved[0], taps[2] + moved[1], moved[2])
            ahead = jnp.concatenate(blocks, axis=0).astype(BF16)
            left = jnp.concatenate([taps[2] + moved[1], moved[2]], axis=0)
            right = jnp.concatenate([taps[0], taps[1] + moved[0]], axis=0)
            back = jnp.concatenate([left.T, right.T], axis=0).astype(BF16)
            for plane in range(2):
                lanes = slice(128 * plane, 128 * plane + 128)
                at = (kz + plane) * 768 + ky * 256
                forward[at : at + 256, lanes] = ahead
                at = (2 - kz + plane) * 768 + (2 - ky) * 256
                backward[at : at + 256, lanes] = back


def convolve(spread_field, band, out):
    for pair in range(2):
        at = pair * 2 * PLANE
        cells = jnp.concatenate([spread_field[at + j * PLANE : at + (j + 1) * PLANE, :] for j in range(4)], axis=1)
        rounded = jnp.dot(cells, band[...], preferred_element_type=F32).astype(BF16)
        for plane in range(2):
            for g in range(32):
                out[2 * pair + plane, :, 128 * g : 128 * g + 128] = rounded[
                    16 * g : 16 * g + 16, 128 * plane : 128 * plane + 128
                ]


def step_kernel(
    act, cot, par, one, two, result, input_grad, new_par, new_one, new_two,
    act_pad, cot_pad, share, row, rows, wide,
    a3, b3, turned, total, flat, forward, backward,
    shares, got, mine, sent, parts, terms, term_parts,
    local, come, hs, gx, gy, gz, gc, rc, rz, rx,
):
    me = place()
    barrier = pltpu.get_barrier_semaphore()
    peers = (
        [slab_peer(me, 1), slab_peer(me, 7)]
        + [x_peer(me, d) for d in X]
        + [z_peer(me, d) for d in (2, 6, 1, 7)]
        + [y_peer(me, d) for d in (2, 6, 1, 7)]
        + [core_peer(me)]
    )
    loads = start([
        pltpu.make_async_copy(par, share.at[0], local.at[0]),
        pltpu.make_async_copy(cot, cot_pad.at[pl.ds(1, 4)], local.at[1]),
        pltpu.make_async_copy(act, act_pad.at[pl.ds(1, 4)], local.at[2]),
        pltpu.make_async_copy(one, share.at[1], local.at[3]),
        pltpu.make_async_copy(two, share.at[2], local.at[4]),
    ])
    for peer in peers:
        pl.semaphore_signal(barrier, inc=1, device_id=peer, device_id_type=MESH)

    def greet(axis):
        for d in (2, 6):
            peer = (y_peer, z_peer)[axis](me, d)
            pl.semaphore_signal(come.at[axis], inc=1, device_id=peer, device_id_type=MESH)

    def greeted(axis):
        pl.semaphore_wait(come.at[axis], 2)

    def inner(pad, out):
        @pl.loop(1, 5)
        def _(p):
            spread(pad, out, p)

    def edges(pad, out):
        @pl.loop(0, 2)
        def _(k):
            spread(pad, out, 5 * k, me["slab"] != 7 * k)

    row[...] = jnp.zeros_like(row)
    loads[0].wait()
    row[0, :, 0:SHARE] = share[0]
    rows[me["z_row"], me["x"]] = row[0]
    loads[1].wait()
    inner(cot_pad, b3)
    loads[2].wait()
    for p in range(1, 5):
        turn(act_pad, turned, p)
    pl.semaphore_wait(barrier, len(peers))

    own = rows.at[me["z_row"], me["x"]]
    gather_x = start([remote(row.at[0], own, gx, k, x_peer(me, d)) for k, d in enumerate(X)])
    greet(1)
    cot_halo = start([
        remote(cot_pad.at[4], cot_pad.at[0], hs, 0, slab_peer(me, 1)),
        remote(cot_pad.at[1], cot_pad.at[5], hs, 1, slab_peer(me, 7)),
    ])
    kernel_gradient(turned, b3, total, (2, 3, 1, 4))
    fold(total, flat, (1,))
    wait_recv(gather_x)
    greet(0)
    greeted(1)
    four = rows.at[me["z_row"]]
    gather_z = start([remote(four, four, gz, k, z_peer(me, d)) for k, d in enumerate(EIGHT)])
    inner(act_pad, a3)
    loads[3].wait()
    loads[4].wait()
    wait_recv(cot_halo)
    act_halo = start([
        remote(act_pad.at[4], act_pad.at[0], hs, 2, slab_peer(me, 1)),
        remote(act_pad.at[1], act_pad.at[5], hs, 3, slab_peer(me, 7)),
    ])
    edges(cot_pad, b3)
    kernel_gradient(turned, b3, total, (0, 5))
    fold(total, flat, (0, 2))
    sum_core = []
    for zh in range(2):
        to_shares(flat, shares, zh)
        half = pl.ds(4 * zh, 4)
        sum_core += start([remote(shares.at[1 - me["core"], half], got.at[half], rc, zh, core_peer(me))])
    greeted(0)
    wait_recv(gather_z)
    wide[me["core"], me["y"]] = jnp.concatenate([rows[k // 4, k % 4] for k in range(32)], axis=0).astype(BF16)
    block = wide.at[me["core"], me["y"]]
    gather_y = start([remote(block, block, gy, k, y_peer(me, d)) for k, d in enumerate(EIGHT)])
    gather_core = start([remote(block, block, gc, 7, core_peer(me))])
    for k in range(8):
        if k % 4 == 0:
            wait_recv([sum_core[k // 4]])
        both = shares[me["core"], k] + got[k]
        mine[k] = both
        sent[k] = both.astype(BF16)
    sum_z = start([
        remote(sent.at[(me["z"] + d) % 8], parts.at[k], rz, k, z_peer(me, d)) for k, d in enumerate(EIGHT)
    ])

    wait_recv(act_halo)
    edges(act_pad, a3)

    for k in reversed(range(7)):
        wait_recv([gather_y[k]])
        landed = wide.at[me["core"], (me["y"] + 8 - EIGHT[k]) % 8]
        gather_core += start([remote(landed, landed, gc, k, core_peer(me))])
    wait_recv(sum_z)
    summed = mine[me["z"]]
    for k in range(7):
        summed = summed + parts[k].astype(F32)
    for k in range(32):
        terms[k] = summed[k : k + 1, :]
    sum_xy = [remote(terms.at[xy_row(me, o)], term_parts.at[k], rx, 0, xy_peer(me, o)) for k, o in enumerate(XY)]
    start(sum_xy)
    all_xy = remote(term_parts, term_parts, rx, 0, xy_peer(me, XY[0]))
    wait_recv(gather_core)
    from_shares(wide, flat)
    bands(flat, forward, backward)
    convolve(a3, forward, result)
    convolve(b3, backward, input_grad)

    wait_send(cot_halo + gather_x + gather_y + act_halo + gather_z + sum_core + sum_z + gather_core)
    wait_recv([all_xy])
    summed = terms[me["row"]]
    for k in range(31):
        summed = summed + term_parts[k]
    scaled = summed[:, 0:SHARE] / jnp.sqrt(F32(64 * 32 * 16 * 64))
    first_moment = 0.9 * share[1] + 0.1 * scaled
    second_moment = 0.999 * share[2] + 0.001 * scaled * scaled
    change = 3.0 * (first_moment / (1.0 - 0.9**10)) / (jnp.sqrt(second_moment / (1.0 - 0.999**10)) + 1e-08)
    new_par[...] = share[0] - change
    new_one[...] = first_moment
    new_two[...] = second_moment
    wait_send([all_xy])


def step(act, cot, par, one, two):
    vmem, hbm = pl.BlockSpec(memory_space=pltpu.VMEM), pl.BlockSpec(memory_space=pltpu.HBM)
    planes = jax.ShapeDtypeStruct((4, 16, 4096), BF16)
    share = jax.ShapeDtypeStruct((1, SHARE), F32)
    return pl.pallas_call(
        step_kernel,
        out_shape=(planes, planes) + (share,) * 3,
        in_specs=[hbm] * 5,
        out_specs=(vmem,) * 5,
        scratch_shapes=[
            pltpu.VMEM((6, 16, 4096), BF16),
            pltpu.VMEM((6, 16, 4096), BF16),
            pltpu.VMEM((3, 1, SHARE), F32),
            pltpu.VMEM((1, 1, 256), F32),
            pltpu.VMEM((8, 4, 1, 256), F32),
            pltpu.VMEM((2, 8, 32, 256), BF16),
            pltpu.VMEM((6 * PLANE, 768), BF16),
            pltpu.VMEM((6 * PLANE, 768), BF16),
            pltpu.VMEM((512, 512), BF16),
            pltpu.VMEM((384, 768), F32),
            pltpu.VMEM((1728, 128), F32),
            pltpu.VMEM((3072, 256), BF16),
            pltpu.VMEM((3072, 256), BF16),
            pltpu.VMEM((2, 8, 32, 256), F32),
            pltpu.VMEM((8, 32, 256), F32),
            pltpu.VMEM((8, 32, 256), F32),
            pltpu.VMEM((8, 32, 256), BF16),
            pltpu.VMEM((7, 32, 256), BF16),
            pltpu.VMEM((32, 1, 256), F32),
            pltpu.VMEM((31, 1, 256), F32),
            pltpu.SemaphoreType.DMA((5,)),
            pltpu.SemaphoreType.REGULAR((2,)),
            pltpu.SemaphoreType.DMA((2, 4)),
            pltpu.SemaphoreType.DMA((2, 3)),
            pltpu.SemaphoreType.DMA((2, 7)),
            pltpu.SemaphoreType.DMA((2, 7)),
            pltpu.SemaphoreType.DMA((2, 8)),
            pltpu.SemaphoreType.DMA((2, 2)),
            pltpu.SemaphoreType.DMA((2, 7)),
            pltpu.SemaphoreType.DMA((2, 1)),
        ],
        compiler_params=pltpu.CompilerParams(
            collective_id=0, has_side_effects=True, vmem_limit_bytes=int(VMEM_MIB * 2**20)
        ),
    )(act, cot, par, one, two)


def place_kernel(*refs):
    sems = refs[-1]
    pairs = [(refs[k].at[z], refs[k + 5].at[z]) for z in range(4) for k in range(2)]
    pairs += [(refs[k], refs[k + 5]) for k in range(2, 5)]
    copies = start([pltpu.make_async_copy(a, b, sems.at[n]) for n, (a, b) in enumerate(pairs)])
    for copy in copies:
        copy.wait()


def place_outputs(*arrays):
    hbm = pl.BlockSpec(memory_space=pltpu.HBM)
    return pl.pallas_call(
        place_kernel,
        out_shape=tuple(jax.ShapeDtypeStruct(a.shape, a.dtype) for a in arrays),
        in_specs=[hbm] * 5,
        out_specs=(hbm,) * 5,
        scratch_shapes=[pltpu.SemaphoreType.DMA((11,))],
        compiler_params=pltpu.CompilerParams(vmem_limit_bytes=8 * 2**20),
    )(*arrays)


def on_device(activations, cotangent, params, moment_one, moment_two):
    par, one, two = (a.reshape(1, SHARE) for a in (params, moment_one, moment_two))
    outputs = step(activations[0], cotangent[0], par, one, two)
    result, input_grad, new_par, new_one, new_two = place_outputs(*outputs)
    return (
        result[None],
        input_grad[None],
        new_par.reshape(SHARE),
        new_one.reshape(SHARE),
        new_two.reshape(SHARE),
    )


def solution(mesh):
    field, share = P("dp", "slab", None, None), P(("slab", "dp"))
    return jax.shard_map(
        on_device,
        mesh=mesh,
        in_specs=(field, field, share, share, share),
        out_specs=(field, field, share, share, share),
        check_vma=False,
    )
```
